256 devices in a mesh: dp: 16 (over y_hi, z), head: 16 (over x, y_lo, core).
Axes of the slice: x: 4, y: 4 (y_hi: 2, y_lo: 2; y = y_hi * 2 + y_lo), z: 8, core: 2. Of those that a mesh axis runs over, the one named last changes fastest.
Arguments:
- tokens: bfloat16 [10240, 7168], P('dp', 'head'), may hold values from -40 to 40
- query_latent: bfloat16 [10240, 1536], P('dp'), may hold values from -20 to 20
- keyval_latent: bfloat16 [10240, 512], P('dp'), may hold values from -20 to 20
- query_gain: float32 [1536], replicated, may hold values from 0.5 to 12
- keyval_gain: float32 [512], replicated, may hold values from 0.5 to 12
- query_cotangent: bfloat16 [10240, 24576], P('dp', 'head'), may hold values from -20 to 20
- keyval_cotangent: bfloat16 [10240, 32768], P('dp', 'head'), may hold values from -20 to 20
- master_query_up: float32 [1536, 24576], P('dp', 'head'), may hold values from -0.15625 to 0.15625
- master_keyval_up: float32 [512, 32768], P('dp', 'head'), may hold values from -0.25 to 0.25
- master_query_down: float32 [1536, 7168], P('dp', 'head'), may hold values from -0.0625 to 0.0625
- master_keyval_down: float32 [512, 7168], P('dp', 'head'), may hold values from -0.0625 to 0.0625
- mean_query_up: float32 [1536, 24576], P('dp', 'head'), may hold values from -0.15625 to 0.15625
- mean_keyval_up: float32 [512, 32768], P('dp', 'head'), may hold values from -0.15625 to 0.15625
- mean_query_down: float32 [1536, 7168], P('dp', 'head'), may hold values from -0.75 to 0.75
- mean_keyval_down: float32 [512, 7168], P('dp', 'head'), may hold values from -0.75 to 0.75
- square_query_up: float32 [128], P('head'), may hold values from 0.0001 to 0.001
- square_keyval_up: float32 [128], P('head'), may hold values from 0.0001 to 0.001
- square_query_down: float32 [1536], P('dp'), may hold values from 0.003 to 0.1
- square_keyval_down: float32 [512], P('dp'), may hold values from 0.003 to 0.1
Outputs:
- token_grad: bfloat16 [10240, 7168], P('dp', 'head')
- update_query_up: float32 [1536, 24576], P('dp', 'head')
- update_keyval_up: float32 [512, 32768], P('dp', 'head')
- update_query_down: float32 [1536, 7168], P('dp', 'head')
- update_keyval_down: float32 [512, 7168], P('dp', 'head')
- mean_query_up_next: float32 [1536, 24576], P('dp', 'head')
- mean_keyval_up_next: float32 [512, 32768], P('dp', 'head')
- mean_query_down_next: float32 [1536, 7168], P('dp', 'head')
- mean_keyval_down_next: float32 [512, 7168], P('dp', 'head')
- square_query_up_next: float32 [128], P('head')
- square_keyval_up_next: float32 [128], P('head')
- square_query_down_next: float32 [1536], P('dp')
- square_keyval_down_next: float32 [512], P('dp')
The draws below stay inside these ranges and needn't reach their ends.
All inputs are finite; a program needn't handle non-finite values.
Results may differ from the reference program's by a relative error of at most 0.024.
Values may be sent and summed in bfloat16 or wider, within the bound.
A program may use at most 128 MiB of HBM per device.

```python
import math
import jax
import jax.numpy as jnp
from jax import lax

D = 7168
H = 128
QL = 1536
KVL = 512
QK = 192
KVH = 256
TOK_DEV = 640
TOKENS = 10240
N_DP = 16


def spread_factors(key, count, lower, upper):
    return jnp.exp(jax.random.uniform(key, (count,), jnp.float32, math.log(lower), math.log(upper)))


def rising(count, top):
    return 1.0 + (top - 1.0) * jnp.arange(count, dtype=jnp.float32) / max(count - 1, 1)


def top_factor():
    return 3.0


def drawn_field(keys, rows, cols):
    return jnp.clip(jax.random.normal(keys[1], (rows, cols), jnp.float32), -6.0, 6.0)


def rough_field(key, rows, cols, lower, upper, bound):
    keys = jax.random.split(key, 4)
    column_scale = spread_factors(keys[0], cols, lower, upper)
    values = drawn_field(keys, rows, cols)
    return jnp.clip(values * column_scale[None, :], -bound, bound)


def draw_tokens(key, part):
    field = rough_field(key, TOKENS, D, 0.4, 2.5, 40.0)
    return jnp.clip(field * rising(D, top_factor())[None, :], -40.0, 40.0).astype(jnp.bfloat16)


def draw_query_latent(key, part):
    return rough_field(key, TOKENS, QL, 0.3, 3.0, 20.0).astype(jnp.bfloat16)


def draw_keyval_latent(key, part):
    return rough_field(key, TOKENS, KVL, 0.3, 3.0, 20.0).astype(jnp.bfloat16)


def draw_query_cotangent(key, part):
    return rough_field(key, TOKENS, H * QK, 0.3, 3.0, 20.0).astype(jnp.bfloat16)


def draw_keyval_cotangent(key, part):
    return rough_field(key, TOKENS, H * KVH, 0.3, 3.0, 20.0).astype(jnp.bfloat16)


def draw_query_gain(key, part):
    return spread_factors(key, QL, 0.5, 2.0) * rising(QL, top_factor())


def draw_keyval_gain(key, part):
    return spread_factors(key, KVL, 0.5, 2.0) * rising(KVL, top_factor())


def block_scale(key, extent, cuts, smallest, largest):
    level, own = 1.0, jax.random.fold_in(key, 6)
    for position, blocks in cuts:
        heights = jnp.exp(jax.random.uniform(jax.random.fold_in(own, position), (blocks,), jnp.float32, smallest / len(cuts), largest / len(cuts)))
        level = level * jnp.repeat(heights, extent[position] // blocks).reshape([-1 if axis == position else 1 for axis in range(len(extent))])
    return level


def centred(rng, dims, spread, most, cuts=(), kind=jnp.bfloat16):
    values = spread * jax.random.normal(rng, dims, jnp.float32)
    if cuts:
        values = values * block_scale(rng, dims, cuts, -0.22, 0.18)
    return jnp.clip(values, -most, most).astype(kind)


def setup_inputs(seed: int = 0) -> dict:
    key_of = jax.random.split(jax.random.key(seed), 20)
    return {
        "tokens": draw_tokens(jax.random.fold_in(key_of[19], 71), 0),
        "query_latent": draw_query_latent(jax.random.fold_in(key_of[19], 71), 0),
        "keyval_latent": draw_keyval_latent(jax.random.fold_in(key_of[19], 71), 0),
        "query_gain": draw_query_gain(jax.random.fold_in(key_of[19], 71), 0),
        "keyval_gain": draw_keyval_gain(jax.random.fold_in(key_of[19], 71), 0),
        "query_cotangent": draw_query_cotangent(jax.random.fold_in(key_of[19], 71), 0),
        "keyval_cotangent": draw_keyval_cotangent(jax.random.fold_in(key_of[19], 71), 0),
        "master_query_up": centred(key_of[7], (QL, H * QK), QL ** -0.5, 0.15625, ((0, 16), (1, 16)), jnp.float32),
        "master_keyval_up": centred(key_of[8], (KVL, H * KVH), KVL ** -0.5, 0.25, ((0, 16), (1, 16)), jnp.float32),
        "master_query_down": centred(key_of[9], (QL, D), D ** -0.5, 0.0625, ((0, 16), (1, 16)), jnp.float32),
        "master_keyval_down": centred(key_of[10], (KVL, D), D ** -0.5, 0.0625, ((0, 16), (1, 16)), jnp.float32),
        "mean_query_up": centred(key_of[11], (QL, H * QK), 0.01, 0.15625, ((0, 16), (1, 16)), jnp.float32),
        "mean_keyval_up": centred(key_of[12], (KVL, H * KVH), 0.01, 0.15625, ((0, 16), (1, 16)), jnp.float32),
        "mean_query_down": centred(key_of[13], (QL, D), 0.05, 0.75, ((0, 16), (1, 16)), jnp.float32),
        "mean_keyval_down": centred(key_of[14], (KVL, D), 0.05, 0.75, ((0, 16), (1, 16)), jnp.float32),
        "square_query_up": jnp.clip(jnp.exp(math.log(0.001) - 2.3025852 * jax.random.uniform(key_of[15], (H,), jnp.float32) ** block_scale(key_of[15], (H,), ((0, 16),), -0.2, 0.2)), 0.0001, 0.001),
        "square_keyval_up": jnp.clip(jnp.exp(math.log(0.001) - 2.3025852 * jax.random.uniform(key_of[16], (H,), jnp.float32) ** block_scale(key_of[16], (H,), ((0, 16),), -0.2, 0.2)), 0.0001, 0.001),
        "square_query_down": jnp.clip(jnp.exp(math.log(0.1) - 3.506558 * jax.random.uniform(key_of[17], (QL,), jnp.float32) ** block_scale(key_of[17], (QL,), ((0, 16),), -0.2, 0.2)), 0.003, 0.1),
        "square_keyval_down": jnp.clip(jnp.exp(math.log(0.1) - 3.506558 * jax.random.uniform(key_of[18], (KVL,), jnp.float32) ** block_scale(key_of[18], (KVL,), ((0, 16),), -0.2, 0.2)), 0.003, 0.1),
    }


norm_eps = 1e-06
adam_eps = 1e-08
beta_first = 0.9
beta_second = 0.95
adam_step = 10

def normalize(latent, gain):
    values = latent.astype(jnp.float32)
    inverse = lax.rsqrt(lax.optimization_barrier(jnp.mean(values * values, axis=1, keepdims=True)) + norm_eps)
    normed = (values * inverse * gain).astype(jnp.bfloat16)
    return (values, inverse, normed)

def norm_back(values, inverse, gain, upstream):
    weighted = gain * upstream
    inner = lax.optimization_barrier(jnp.sum(values * weighted, axis=1, keepdims=True)) / values.shape[1]
    return (inverse * weighted - values * inverse ** 3 * inner).astype(jnp.bfloat16)

def group_grad(left, right):
    left_groups = left.reshape(N_DP, TOK_DEV, left.shape[1])
    right_groups = right.reshape(N_DP, TOK_DEV, right.shape[1])

    def accumulate(total, pair):
        partial_sum = jnp.dot(pair[0].T, pair[1], preferred_element_type=jnp.float32)
        rounded = lax.optimization_barrier(partial_sum.astype(jnp.bfloat16))
        return (total + rounded.astype(jnp.float32), None)
    start = jnp.zeros((left.shape[1], right.shape[1]), jnp.float32)
    total, _ = lax.scan(accumulate, start, (left_groups, right_groups))
    return total / TOKENS

def direction(first_next, second_wide):
    first_scale = 1.0 - beta_first ** adam_step
    second_scale = 1.0 - beta_second ** adam_step
    return first_next / first_scale / (jnp.sqrt(second_wide / second_scale) + adam_eps)

def reference(tokens, query_latent, keyval_latent, query_gain, keyval_gain, query_cotangent, keyval_cotangent, master_query_up, master_keyval_up, master_query_down, master_keyval_down, mean_query_up, mean_keyval_up, mean_query_down, mean_keyval_down, square_query_up, square_keyval_up, square_query_down, square_keyval_down):
    query_up = master_query_up.astype(jnp.bfloat16)
    keyval_up = master_keyval_up.astype(jnp.bfloat16)
    query_down = master_query_down.astype(jnp.bfloat16)
    keyval_down = master_keyval_down.astype(jnp.bfloat16)
    query_values, query_inverse, query_normed = normalize(query_latent, query_gain)
    keyval_values, keyval_inverse, keyval_normed = normalize(keyval_latent, keyval_gain)
    query_upstream = jnp.dot(query_cotangent, query_up.T, preferred_element_type=jnp.float32)
    keyval_upstream = jnp.dot(keyval_cotangent, keyval_up.T, preferred_element_type=jnp.float32)
    query_slope = norm_back(query_values, query_inverse, query_gain, query_upstream)
    keyval_slope = norm_back(keyval_values, keyval_inverse, keyval_gain, keyval_upstream)
    token_grad = (jnp.dot(query_slope, query_down, preferred_element_type=jnp.float32) + jnp.dot(keyval_slope, keyval_down, preferred_element_type=jnp.float32)).astype(jnp.bfloat16)
    grad_query_up = group_grad(query_normed, query_cotangent)
    grad_keyval_up = group_grad(keyval_normed, keyval_cotangent)
    grad_query_down = group_grad(query_slope, tokens)
    grad_keyval_down = group_grad(keyval_slope, tokens)
    mean_query_up_next = beta_first * mean_query_up + (1.0 - beta_first) * grad_query_up
    mean_keyval_up_next = beta_first * mean_keyval_up + (1.0 - beta_first) * grad_keyval_up
    mean_query_down_next = beta_first * mean_query_down + (1.0 - beta_first) * grad_query_down
    mean_keyval_down_next = beta_first * mean_keyval_down + (1.0 - beta_first) * grad_keyval_down
    head_query = lax.optimization_barrier(jnp.mean((grad_query_up * grad_query_up).reshape(QL, H, QK), axis=(0, 2)))
    head_keyval = lax.optimization_barrier(jnp.mean((grad_keyval_up * grad_keyval_up).reshape(KVL, H, KVH), axis=(0, 2)))
    row_query = lax.optimization_barrier(jnp.mean(grad_query_down * grad_query_down, axis=1))
    row_keyval = lax.optimization_barrier(jnp.mean(grad_keyval_down * grad_keyval_down, axis=1))
    square_query_up_next = beta_second * square_query_up + (1.0 - beta_second) * head_query
    square_keyval_up_next = beta_second * square_keyval_up + (1.0 - beta_second) * head_keyval
    square_query_down_next = beta_second * square_query_down + (1.0 - beta_second) * row_query
    square_keyval_down_next = beta_second * square_keyval_down + (1.0 - beta_second) * row_keyval
    update_query_up = direction(mean_query_up_next, jnp.repeat(square_query_up_next, QK)[None, :])
    update_keyval_up = direction(mean_keyval_up_next, jnp.repeat(square_keyval_up_next, KVH)[None, :])
    update_query_down = direction(mean_query_down_next, square_query_down_next[:, None])
    update_keyval_down = direction(mean_keyval_down_next, square_keyval_down_next[:, None])
    return (token_grad, update_query_up, update_keyval_up, update_query_down, update_keyval_down, mean_query_up_next, mean_keyval_up_next, mean_query_down_next, mean_keyval_down_next, square_query_up_next, square_keyval_up_next, square_query_down_next, square_keyval_down_next)
```

```python
import jax
import jax.numpy as jnp
from jax import lax
from jax.experimental import pallas as pl
from jax.experimental.pallas import tpu as pltpu
from jax.sharding import PartitionSpec as P

D = 7168
QL = 1536
KVL = 512
QK = 192
KVH = 256
TOKENS = 10240
TOK = 640

NZ = 8
NX = 4
DC = 448
QR, KR, DR = 96, 32, 128
GQ, GK, GW = 4 * QR, 4 * KR, 4 * (QR + KR)
QC, KC = 1536, 2048
SLICE = 80

norm_eps = 1e-06
adam_eps = 1e-08
beta_first = 0.9
beta_second = 0.95
adam_step = 10
first_scale = 1.0 - beta_first**adam_step
second_scale = 1.0 - beta_second**adam_step

MESH = pl.DeviceIdType.MESH
f32 = jnp.float32
bf16 = jnp.bfloat16
N_SEM = 192


def place(rel, d):
    d = d % NZ
    if d == 0 or d == NZ // 2:
        return (0, rel * 2 + (1 if d else 0))
    if d < NZ // 2:
        return (d, rel * 2)
    return (NZ - d, rel * 2 + 1)


def split3(a):
    hi = a.astype(bf16)
    rest = a - hi.astype(f32)
    mid = rest.astype(bf16)
    low = (rest - mid.astype(f32)).astype(bf16)
    return hi, mid, low


def dot(a, b):
    return jnp.dot(a, b, preferred_element_type=f32)


def dot_t(a, b):
    return lax.dot_general(a, b, (((1,), (1,)), ((), ())), preferred_element_type=f32)


def select_dot(a, chosen):
    hi, mid, low = split3(a)
    return dot(hi, chosen) + dot(mid, chosen) + dot(low, chosen)


def loop(count, body):
    def step(i, carry):
        body(i)
        return carry

    lax.fori_loop(0, count, step, 0)


def total(refs, rows):
    parts = [r[rows, :].astype(f32) for r in refs]
    out = parts[0]
    for p in parts[1:]:
        out = out + p
    return out


def add_into(refs, out, start, rows):
    def body(i):
        at = pl.ds(pl.multiple_of(start + i * 16, 16), 16)
        out[at, :] = total(refs, at).astype(out.dtype)

    loop(rows // 16, body)


def kernel(
    tok_h, lq_h, lk_h, gq_ref, gk_ref, cq_h, ck_h,
    mq_h, mk_h, mdq_h, mdk_h, eq_h, ek_h, edq_h, edk_h,
    sq_ref, sk_ref, sdq_ref, sdk_ref,
    tg_h, uq_h, uk_h, udq_h, udk_h, nq_h, nk_h, ndq_h, ndk_h,
    osq_ref, osk_ref, osdq_ref, osdk_ref,
    tok, lq, lk, cq, ck, mq, mk, md, eq, ek, ed,
    wq, wk, wd, pq, pk, pd, yq, yk, yd, zq, zk, zd,
    normq, normk, turned, up, core_in, half, x_in, mine, pair_in, full,
    latent, gains, slope, tg, small, small_pair, small_z, small_row, small_core, small_lo, small_x,
    send_sems, recv_sems, local_sems,
):
    dp = lax.axis_index("dp")
    hd = lax.axis_index("head")
    yh, z = dp // NZ, dp % NZ
    x, yl, c = hd // 4, (hd // 2) % 2, hd % 2

    def z_dev(k):
        return (yh * NZ + (z + k + NZ) % NZ, hd)

    def x_dev(k):
        return (dp, ((x + k + NX) % NX) * 4 + yl * 2 + c)

    other_half = ((1 - yh) * NZ + z, hd)
    other_low = (dp, x * 4 + (1 - yl) * 2 + c)
    other_core = (dp, x * 4 + yl * 2 + 1 - c)
    z_next = (z_dev(1), z_dev(-1))
    x_next = (x_dev(1), x_dev(-1))

    ids = {}
    sent = []

    def remote(key, src, dst, dev):
        i = ids.setdefault(key, len(ids))
        return pltpu.make_async_remote_copy(
            src_ref=src, dst_ref=dst, send_sem=send_sems.at[i], recv_sem=recv_sems.at[i],
            device_id=dev, device_id_type=MESH,
        )

    def send(key, src, dst, dev):
        copy = remote(key, src, dst, dev)
        copy.start()
        sent.append(copy)

    def recv(key, land):
        remote(key, land, land, other_core).wait_recv()

    n_local = [0]

    def fetch(src, dst):
        copy = pltpu.make_async_copy(src, dst, local_sems.at[n_local[0]])
        n_local[0] += 1
        copy.start()
        return copy

    l_mk, l_mq = fetch(mk_h, mk), fetch(mq_h, mq)
    l_lk, l_ck = fetch(lk_h, lk), fetch(ck_h, ck)
    l_lq, l_cq = fetch(lq_h, lq), fetch(cq_h, cq)
    l_md = (fetch(mdq_h, md.at[pl.ds(0, QR)]), fetch(mdk_h, md.at[pl.ds(QR, KR)]))
    l_tok = fetch(tok_h, tok)
    l_eq, l_ek = fetch(eq_h, eq), fetch(ek_h, ek)
    l_ed = (fetch(edq_h, ed.at[pl.ds(0, QR)]), fetch(edk_h, ed.at[pl.ds(QR, KR)]))

    barrier = pltpu.get_barrier_semaphore()
    peers = [z_dev(k) for k in range(1, NZ)] + [x_dev(k) for k in range(1, NX)]
    peers += [other_half, other_low, other_core]
    for dev in peers:
        pl.semaphore_signal(barrier, inc=1, device_id=dev, device_id_type=MESH)

    def round_rows(src, dst, rows):
        def body(i):
            at = pl.ds(pl.multiple_of(i * 16, 16), 16)
            dst[at, :] = src[at, :].astype(bf16)

        loop(rows // 16, body)

    gathered = {"k": (wk, KR), "q": (wq, QR), "d": (wd, DR)}

    def gather_pair(w):
        ref, _ = gathered[w]
        send(("y", w), ref.at[place(0, 0)], ref.at[place(1, 0)], other_half)

    def gather_first(w, rel):
        ref, _ = gathered[w]
        if rel:
            recv(("y", w), ref.at[place(1, 0)])
        for side, sign in ((0, -1), (1, 1)):
            send(("g", w, rel, 1, side), ref.at[place(rel, 0)], ref.at[place(rel, sign)], z_next[side])

    def gather_next(w, rel, step):
        ref, rows = gathered[w]
        h = rows // 2
        for side, sign in ((0, -1), (1, 1)):
            here = ref.at[place(rel, sign * step)]
            if step == 4:
                recv(("g", w, rel, 4, side), here.at[pl.ds(side * h, h)])
                continue
            recv(("g", w, rel, step, side), here)
            there = ref.at[place(rel, sign * (step + 1))]
            if step == 3:
                here, there = here.at[pl.ds(side * h, h)], there.at[pl.ds(side * h, h)]
            send(("g", w, rel, step + 1, side), here, there, z_next[side])

    def own_block(ref, half_of, d):
        return ref.at[half_of * NZ + (z + d) % NZ]

    scattered = {
        "k": (lambda d: own_block(pk, yh, d), lambda d: own_block(pk, 1 - yh, d), yk, zk, KR),
        "q": (lambda d: own_block(pq, yh, d), lambda d: own_block(pq, 1 - yh, d), yq, zq, QR),
        "d": (lambda d: pd.at[place(0, d)], lambda d: pd.at[place(1, d)], yd, zd, DR),
    }

    def scatter_pair(w, d):
        _, theirs, y, _, _ = scattered[w]
        send(("sy", w, d), theirs(d), y.at[d], other_half)

    def scatter_first(w):
        own, _, y, zz, rows = scattered[w]
        h = rows // 2
        recv(("sy", w, 4), y.at[4])
        add_into([own(4), y.at[4]], own(4), 0, rows)
        for side in range(2):
            at = pl.ds(side * h, h)
            send(("s", w, 0, side), own(4).at[at], zz.at[side, 0].at[at], z_next[side])

    def scatter_next(w, step):
        own, _, y, zz, rows = scattered[w]
        h = rows // 2
        for side in range(2):
            d = 3 - step if side == 0 else 5 + step
            recv(("sy", w, d), y.at[d])
            if step == 0:
                came = zz.at[side, 0]
                recv(("s", w, 0, side), came.at[pl.ds(side * h, h)])
                add_into([own(d), y.at[d], came], own(d), side * h, h)
                add_into([own(d), y.at[d]], own(d), (1 - side) * h, h)
            else:
                came = zz.at[side, step]
                recv(("s", w, step, side), came)
                add_into([own(d), y.at[d], came], own(d), 0, rows)
            send(("s", w, step + 1, side), own(d), zz.at[side, step + 1], z_next[side])

    def scatter_last(w):
        own, _, y, zz, _ = scattered[w]
        recv(("sy", w, 0), y.at[0])
        recv(("s", w, 3, 0), zz.at[0, 3])
        recv(("s", w, 3, 1), zz.at[1, 3])
        return [own(0), y.at[0], zz.at[0, 3], zz.at[1, 3]]

    l_mk.wait()
    round_rows(mk, wk.at[place(0, 0)], KR)
    l_mq.wait()
    round_rows(mq, wq.at[place(0, 0)], QR)
    pl.semaphore_wait(barrier, len(peers))
    gather_pair("k")
    gather_first("k", 0)
    gather_pair("q")
    gather_first("q", 0)
    for load in l_md:
        load.wait()
    round_rows(md, wd.at[place(0, 0)], DR)

    def normalize(src, gain_ref, dst, width):
        def body(i):
            at = pl.ds(pl.multiple_of(i * 16, 16), 16)
            values = src[at, :].astype(f32)
            inverse = lax.rsqrt(jnp.sum(values * values, axis=1, keepdims=True) / width + norm_eps)
            dst[at, :] = (values * inverse * gain_ref[...]).astype(bf16)

        loop(TOK // 16, body)

    def turn(src, start, width):
        def body(i):
            at = pl.ds(pl.multiple_of(i * 128, 128), 128)
            block = src[at, pl.ds(start, width)]
            turned[pl.ds(0, width), at] = block.T

        loop(TOK // 128, body)

    def part_keyval(half_of):
        turn(normk, pl.multiple_of(half_of * 256, 128), 256)

        def body(i):
            at = pl.ds(pl.multiple_of(i * 512, 512), 512)
            out = dot(turned[pl.ds(0, 256), :], ck[:, at]).astype(bf16)
            pk[pl.ds(half_of * NZ, NZ), :, at] = out.reshape(NZ, KR, 512)

        loop(KC // 512, body)

    def part_query(half_of):
        def chunk(q):
            turn(normq, pl.multiple_of(half_of * 768 + q * GQ, 128), GQ)

            def body(i):
                at = pl.ds(pl.multiple_of(i * 512, 512), 512)
                out = dot(turned[pl.ds(0, GQ), :], cq[:, at]).astype(bf16)
                pq[pl.ds(half_of * NZ + q * 4, 4), :, at] = out.reshape(4, QR, 512)

            loop(QC // 512, body)

        loop(2, chunk)

    order = (4, 3, 5, 2, 6, 1, 7, 0)
    l_lk.wait()
    normalize(lk, gk_ref, normk, KVL)
    l_ck.wait()
    part_keyval(1 - yh)
    for d in order[:3]:
        scatter_pair("k", d)
    l_lq.wait()
    normalize(lq, gq_ref, normq, QL)
    gather_first("k", 1)
    l_cq.wait()
    part_query(1 - yh)
    gather_first("q", 1)
    for i, d in enumerate(order):
        scatter_pair("q", d)
        if i >= 3:
            scatter_pair("k", d)
    gather_pair("d")
    part_keyval(yh)
    part_query(yh)

    first_token = pl.multiple_of(c * (TOK // 2) + x * SLICE, 16)

    def arrange(src, gain_ref, rows, natural, width, group, at):
        lane = lax.broadcasted_iota(jnp.int32, (1, 4 * rows), 1)
        j = sum((lane >= rows * k).astype(jnp.int32) for k in (1, 2, 3))
        inside = lane - j * rows
        rel, back = j // 2, j % 2
        d = back * (NZ // 2) if group == 0 else jnp.where(back == 1, NZ - group, group)
        owner = jnp.where(rel == 1, 1 - yh, yh) * NZ + (z + d) % NZ
        source = owner * rows + inside
        chosen = (lax.broadcasted_iota(jnp.int32, (width, 4 * rows), 0) == source).astype(f32).astype(bf16)
        latent[group, :, at] = dot(src[pl.ds(first_token, SLICE), :], chosen)
        gain = jnp.broadcast_to(gain_ref[...], (8, width))
        gains[group, :, at] = select_dot(gain, chosen)

    for g in range(4):
        arrange(lq, gq_ref, QR, 0, QL, g, pl.ds(0, GQ))
        arrange(lk, gk_ref, KR, 0, KVL, g, pl.ds(GQ, GK))

    def upstream(g):
        def body(i):
            at = pl.ds(pl.multiple_of(i * 160, 160), 160)
            up[g, at, pl.ds(0, GQ)] = dot_t(cq[at, :], wq[g].reshape(GQ, QC)).astype(bf16)
            up[g, at, pl.ds(GQ, GK)] = dot_t(ck[at, :], wk[g].reshape(GK, KC)).astype(bf16)

        loop(TOK // 160, body)
        there = pl.ds(pl.multiple_of((1 - c) * 320, 16), 320)
        send(("c", g), up.at[g, there], core_in.at[g], other_core)

    def after_core(g):
        recv(("c", g), core_in.at[g])
        here = up.at[g, pl.ds(pl.multiple_of(c * 320, 16), 320)]
        add_into([here, core_in.at[g]], half.at[g], 0, 320)
        for k in (2, 1, 3):
            to = (x + k) % NX
            send(("x", g, k), half.at[g, pl.ds(pl.multiple_of(to * SLICE, 16), SLICE)], x_in.at[g, k - 1], x_dev(k))

    def after_x(g):
        for k in range(1, NX):
            recv(("x", g, k), x_in.at[g, k - 1])
        here = half.at[g, pl.ds(pl.multiple_of(x * SLICE, 16), SLICE)]
        add_into([here] + [x_in.at[g, k] for k in range(NX - 1)], mine.at[g], 0, SLICE)
        send(("l", g), mine.at[g], pair_in.at[g], other_low)

    def after_low(g):
        recv(("l", g), pair_in.at[g])
        add_into([mine.at[g], pair_in.at[g]], full.at[g], 0, SLICE)

    for step in (1, 2, 3):
        for rel in range(2):
            for w in ("k", "q"):
                gather_next(w, rel, step)
        upstream(step)
        if step > 1:
            after_x(step - 1)
        if step > 2:
            after_low(step - 2)
        after_core(step)

    after_x(3)
    after_low(2)
    for w in ("k", "q"):
        gather_next(w, 0, 4)
    scatter_first("k")
    for w in ("k", "q"):
        gather_next(w, 1, 4)
    scatter_first("q")
    upstream(0)
    gather_first("d", 0)
    gather_first("d", 1)
    after_low(3)
    scatter_next("k", 0)
    after_core(0)
    scatter_next("q", 0)
    for rel in range(2):
        gather_next("d", rel, 1)
    after_x(0)
    scatter_next("k", 1)
    after_low(0)

    own_rows = pl.ds(first_token, SLICE)

    def norm_back(i):
        at = pl.ds(pl.multiple_of(i * 16, 16), 16)
        to = pl.ds(pl.multiple_of(first_token + i * 16, 16), 16)
        for first, width, units in ((0, GQ, QL), (GQ, GK, KVL)):
            cols = pl.ds(first, width)
            squares = 0.0
            inner = 0.0
            for g in range(4):
                values = latent[g, at, cols]
                squares += jnp.sum(values * values, axis=1, keepdims=True)
                inner += jnp.sum(values * gains[g, pl.ds(0, 1), cols] * full[g, at, cols], axis=1, keepdims=True)
            inverse = lax.rsqrt(squares / units + norm_eps)
            scale = inverse * inverse * inverse * (inner / units)
            for g in range(4):
                weighted = gains[g, pl.ds(0, 1), cols] * full[g, at, cols]
                slope[to, pl.ds(g * GW + first, width)] = (inverse * weighted - latent[g, at, cols] * scale).astype(bf16)

    loop(SLICE // 16, norm_back)

    sides = (pl.ds(0, 2 * GW), pl.ds(2 * GW, 2 * GW))

    def block_rows(k, core):
        return pl.ds(pl.multiple_of(core * 320 + ((x + k + NX) % NX) * SLICE, 16), SLICE)

    for part in range(2):
        for side in range(2):
            cols = sides[part if side == 0 else 1 - part]
            view = slope.at[own_rows, cols]
            send(("a", 1, side, part), view, view, x_next[side])
    view = slope.at[own_rows, :]
    send(("ac", 0), view, view, other_core)
    scatter_next("q", 1)
    for side, back in ((0, -1), (1, 1)):
        view = slope.at[block_rows(back, c), sides[side]]
        recv(("a", 1, side, 0), view)
        send(("a", 2, side), view, view, x_next[side])
    for rel in range(2):
        gather_next("d", rel, 2)
    scatter_next("k", 2)
    for side, back in ((0, -1), (1, 1)):
        recv(("a", 1, side, 1), slope.at[block_rows(back, c), sides[1 - side]])
        view = slope.at[block_rows(back, c), :]
        send(("ac", 1 + side), view, view, other_core)
    for side in range(2):
        recv(("a", 2, side), slope.at[block_rows(2, c), sides[side]])
    view = slope.at[block_rows(2, c), :]
    send(("ac", 3), view, view, other_core)
    for i, k in enumerate((0, -1, 1, 2)):
        recv(("ac", i), slope.at[block_rows(k, 1 - c), :])

    l_tok.wait()
    for g in range(4):
        turn(slope, g * GW, GW)
        out = dot_t(turned[...], tok[...]).astype(bf16)
        pd[g, :, pl.ds(0, QR), :] = out[:GQ].reshape(4, QR, DC)
        pd[g, :, pl.ds(QR, KR), :] = out[GQ:].reshape(4, KR, DC)
    for d in order:
        scatter_pair("d", d)
    scatter_next("q", 2)
    for rel in range(2):
        gather_next("d", rel, 3)

    def finish(refs, grad, mean, rows, cols):
        def step(i, squares):
            at = pl.ds(pl.multiple_of(i * 16, 16), 16)
            g = total(refs, at) / TOKENS
            mean[at, :] = beta_first * mean[at, :] + (1.0 - beta_first) * g
            return squares + g[0:8] * g[0:8] + g[8:16] * g[8:16]

        return lax.fori_loop(0, rows // 16, step, jnp.zeros((8, cols), f32))

    def heads_of(width, per_head):
        col = lax.broadcasted_iota(jnp.int32, (width, 128), 0)
        head = lax.broadcasted_iota(jnp.int32, (width, 128), 1)
        return ((col >= head * per_head) & (col < (head + 1) * per_head)).astype(f32).astype(bf16)

    def columns_of(width, per_head):
        head = lax.broadcasted_iota(jnp.int32, (128, width), 0)
        col = lax.broadcasted_iota(jnp.int32, (128, width), 1)
        return ((col >= head * per_head) & (col < (head + 1) * per_head)).astype(f32).astype(bf16)

    l_ek.wait()
    squares_k = finish(scatter_last("k"), None, ek, KR, KC)
    heads_k = jnp.sum(select_dot(squares_k, heads_of(KC, KVH)), axis=0, keepdims=True) / (KVL * KVH)
    scatter_first("d")
    l_eq.wait()
    squares_q = finish(scatter_last("q"), None, eq, QR, QC)
    heads_q = jnp.sum(select_dot(squares_q, heads_of(QC, QK)), axis=0, keepdims=True) / (QL * QK)
    row8 = lax.broadcasted_iota(jnp.int32, (8, 128), 0)
    small[...] = jnp.where(row8 == 0, heads_q, jnp.where(row8 == 1, heads_k, 0.0))
    send(("hy",), small, small_pair, other_half)
    scatter_next("d", 0)
    recv(("hy",), small_pair)
    small_z[0] = small[...] + small_pair[...]
    for k in range(1, NZ):
        send(("hz", k), small_z.at[0], small_z.at[k], z_dev(k))

    for rel in range(2):
        gather_next("d", rel, 4)

    def token_grad(i):
        at = pl.ds(pl.multiple_of(i * 128, 128), 128)
        out = jnp.zeros((128, DC), f32)
        for g in range(4):
            out += dot(slope[at, pl.ds(g * GW, GQ)], wd[g, :, pl.ds(0, QR), :].reshape(GQ, DC))
            out += dot(slope[at, pl.ds(g * GW + GQ, GK)], wd[g, :, pl.ds(QR, KR), :].reshape(GK, DC))
        tg[:, at] = out.T.astype(bf16)

    loop(TOK // 128, token_grad)
    stores = [fetch(tg, tg_h)]
    scatter_next("d", 1)

    for k in range(1, NZ):
        recv(("hz", k), small_z.at[k])
    heads = small_z[0]
    for k in range(1, NZ):
        heads = heads + small_z[k]
    small_row[...] = jnp.zeros((8, 128), f32)
    small_row[pl.ds(0, 1), pl.ds(0, 8)] = sq_ref[...]
    small_row[pl.ds(1, 1), pl.ds(0, 8)] = sk_ref[...]
    second = beta_second * small_row[...] + (1.0 - beta_second) * heads
    osq_ref[...] = second[0:1, 0:8]
    osk_ref[...] = second[1:2, 0:8]

    def update(second_wide, mean, out, rows):
        factor = 1.0 / (jnp.sqrt(second_wide / second_scale) + adam_eps)

        def body(i):
            at = pl.ds(pl.multiple_of(i * 16, 16), 16)
            out[at, :] = mean[at, :] / first_scale * factor

        loop(rows // 16, body)

    update(select_dot(second, columns_of(QC, QK))[0:1], eq, mq, QR)
    update(select_dot(second, columns_of(KC, KVH))[1:2], ek, mk, KR)
    stores += [fetch(eq, nq_h), fetch(ek, nk_h), fetch(mq, uq_h), fetch(mk, uk_h)]

    scatter_next("d", 2)
    eye = lax.broadcasted_iota(jnp.int32, (128, 128), 0) == lax.broadcasted_iota(jnp.int32, (128, 128), 1)
    small_row[...] = jnp.zeros((8, 128), f32)
    small_row[pl.ds(0, 1), pl.ds(0, QR)] = sdq_ref[...]
    small_row[pl.ds(0, 1), pl.ds(QR, KR)] = sdk_ref[...]
    old = small_row[pl.ds(0, 1), :]
    for load in l_ed:
        load.wait()
    grad = total(scatter_last("d"), slice(None)) / TOKENS
    mean_next = beta_first * ed[...] + (1.0 - beta_first) * grad
    ed[...] = mean_next
    column = jnp.sum(grad * grad, axis=1, keepdims=True) / D
    row = jnp.sum(jnp.where(eye, column, 0.0), axis=0, keepdims=True)
    small_core[0] = jnp.broadcast_to(row, (8, 128))
    send(("rc",), small_core.at[0], small_core.at[1], other_core)
    stores += [fetch(ed.at[pl.ds(0, QR)], ndq_h), fetch(ed.at[pl.ds(QR, KR)], ndk_h)]
    recv(("rc",), small_core.at[1])
    small_lo[0] = small_core[0] + small_core[1]
    send(("rl",), small_lo.at[0], small_lo.at[1], other_low)
    recv(("rl",), small_lo.at[1])
    small_x[0] = small_lo[0] + small_lo[1]
    for k in range(1, NX):
        send(("rx", k), small_x.at[0], small_x.at[k], x_dev(k))
    for k in range(1, NX):
        recv(("rx", k), small_x.at[k])
    rows_total = (small_x[0] + small_x[1]) + (small_x[2] + small_x[3])
    second_row = beta_second * old + (1.0 - beta_second) * rows_total[0:1]
    osdq_ref[...] = second_row[:, 0:QR]
    osdk_ref[...] = second_row[:, QR:DR]
    second_col = jnp.sum(jnp.where(eye, second_row, 0.0), axis=1, keepdims=True)
    factor = 1.0 / (jnp.sqrt(second_col / second_scale) + adam_eps)
    md[...] = mean_next / first_scale * factor
    stores += [fetch(md.at[pl.ds(0, QR)], udq_h), fetch(md.at[pl.ds(QR, KR)], udk_h)]

    for copy in sent:
        copy.wait_send()
    for store in stores:
        store.wait()


def local(*args):
    (
        tokens, query_latent, keyval_latent, query_gain, keyval_gain, query_cotangent, keyval_cotangent,
        master_query_up, master_keyval_up, master_query_down, master_keyval_down,
        mean_query_up, mean_keyval_up, mean_query_down, mean_keyval_down,
        square_query_up, square_keyval_up, square_query_down, square_keyval_down,
    ) = args
    hbm = pl.BlockSpec(memory_space=pl.ANY)
    vmem = pl.BlockSpec(memory_space=pltpu.VMEM)

    def shape(rows, cols, kind=f32):
        return jax.ShapeDtypeStruct((rows, cols), kind)

    V = pltpu.VMEM
    outs = pl.pallas_call(
        kernel,
        name="backward_and_update",
        out_shape=(
            shape(DC, TOK, bf16),
            shape(QR, QC), shape(KR, KC), shape(QR, DC), shape(KR, DC),
            shape(QR, QC), shape(KR, KC), shape(QR, DC), shape(KR, DC),
            shape(1, 8), shape(1, 8), shape(1, QR), shape(1, KR),
        ),
        in_specs=[hbm] * 3 + [vmem] * 2 + [hbm] * 10 + [vmem] * 4,
        out_specs=(hbm,) * 9 + (vmem,) * 4,
        scratch_shapes=[
            V((DC, TOK), bf16), V((TOK, QL), bf16), V((TOK, KVL), bf16), V((TOK, QC), bf16), V((TOK, KC), bf16),
            V((QR, QC), f32), V((KR, KC), f32), V((DR, DC), f32),
            V((QR, QC), f32), V((KR, KC), f32), V((DR, DC), f32),
            V((4, 4, QR, QC), bf16), V((4, 4, KR, KC), bf16), V((4, 4, DR, DC), bf16),
            V((16, QR, QC), bf16), V((16, KR, KC), bf16), V((4, 4, DR, DC), bf16),
            V((8, QR, QC), bf16), V((8, KR, KC), bf16), V((8, DR, DC), bf16),
            V((2, 4, QR, QC), bf16), V((2, 4, KR, KC), bf16), V((2, 4, DR, DC), bf16),
            V((TOK, QL), bf16), V((TOK, KVL), bf16), V((GW, TOK), bf16),
            V((4, TOK, GW), bf16), V((4, 320, GW), bf16), V((4, 320, GW), bf16),
            V((4, 3, SLICE, GW), bf16), V((4, SLICE, GW), bf16), V((4, SLICE, GW), bf16), V((4, SLICE, GW), f32),
            V((4, SLICE, GW), f32), V((4, 8, GW), f32),
            V((TOK, 4 * GW), bf16), V((DC, TOK), bf16),
            V((8, 128), f32), V((8, 128), f32), V((8, 8, 128), f32), V((8, 128), f32),
            V((2, 8, 128), f32), V((2, 8, 128), f32), V((4, 8, 128), f32),
            pltpu.SemaphoreType.DMA((N_SEM,)), pltpu.SemaphoreType.DMA((N_SEM,)), pltpu.SemaphoreType.DMA((32,)),
        ],
        compiler_params=pltpu.CompilerParams(
            collective_id=0, has_side_effects=True, vmem_limit_bytes=62 * 2**20
        ),
        cost_estimate=pl.CostEstimate(flops=11 * 10**9, bytes_accessed=14 * 10**6, transcendentals=0),
    )(
        tokens.T, query_latent, keyval_latent, query_gain.reshape(1, QL), keyval_gain.reshape(1, KVL),
        query_cotangent, keyval_cotangent,
        master_query_up, master_keyval_up, master_query_down, master_keyval_down,
        mean_query_up, mean_keyval_up, mean_query_down, mean_keyval_down,
        square_query_up.reshape(1, 8), square_keyval_up.reshape(1, 8),
        square_query_down.reshape(1, QR), square_keyval_down.reshape(1, KR),
    )
    return (
        outs[0].T, *outs[1:9],
        outs[9].reshape(8), outs[10].reshape(8), outs[11].reshape(QR), outs[12].reshape(KR),
    )


def solution(mesh):
    both = P("dp", "head")
    return jax.shard_map(
        local,
        mesh=mesh,
        in_specs=(both, P("dp", None), P("dp", None), P(), P()) + (both,) * 10
        + (P("head"), P("head"), P("dp"), P("dp")),
        out_specs=(both,) * 9 + (P("head"), P("head"), P("dp"), P("dp")),
        check_vma=False,
    )
```

```python
import jax
import jax.numpy as jnp
from jax import lax
from jax.experimental import pallas as pl
from jax.experimental.pallas import tpu as pltpu
from jax.sharding import PartitionSpec as P

D = 7168
QL = 1536
KVL = 512
QK = 192
KVH = 256
TOKENS = 10240
TOK = 640

NZ = 8
NX = 4
DC = 448
QR, KR, DR = 96, 32, 128
GQ, GK, GW = 4 * QR, 4 * KR, 4 * (QR + KR)
QC, KC = 1536, 2048
SLICE = 80

norm_eps = 1e-06
adam_eps = 1e-08
beta_first = 0.9
beta_second = 0.95
adam_step = 10
first_scale = 1.0 - beta_first**adam_step
second_scale = 1.0 - beta_second**adam_step

MESH = pl.DeviceIdType.MESH
f32 = jnp.float32
bf16 = jnp.bfloat16
N_SEM = 192


def place(rel, d):
    d = d % NZ
    if d == 0 or d == NZ // 2:
        return (0, rel * 2 + (1 if d else 0))
    if d < NZ // 2:
        return (d, rel * 2)
    return (NZ - d, rel * 2 + 1)


def split3(a):
    hi = a.astype(bf16)
    rest = a - hi.astype(f32)
    mid = rest.astype(bf16)
    low = (rest - mid.astype(f32)).astype(bf16)
    return hi, mid, low


def dot(a, b):
    return jnp.dot(a, b, preferred_element_type=f32)


def dot_t(a, b):
    return lax.dot_general(a, b, (((1,), (1,)), ((), ())), preferred_element_type=f32)


def select_dot(a, chosen):
    hi, mid, low = split3(a)
    return dot(hi, chosen) + dot(mid, chosen) + dot(low, chosen)


def loop(count, body):
    def step(i, carry):
        body(i)
        return carry

    lax.fori_loop(0, count, step, 0)


def total(refs, rows):
    parts = [r[rows, :].astype(f32) for r in refs]
    out = parts[0]
    for p in parts[1:]:
        out = out + p
    return out


def add_into(refs, out, start, rows):
    def body(i):
        at = pl.ds(pl.multiple_of(start + i * 16, 16), 16)
        out[at, :] = total(refs, at).astype(out.dtype)

    loop(rows // 16, body)


def kernel(
    tok_h, lq_h, lk_h, gq_ref, gk_ref, cq_h, ck_h,
    mq_h, mk_h, mdq_h, mdk_h, eq_h, ek_h, edq_h, edk_h,
    sq_ref, sk_ref, sdq_ref, sdk_ref,
    tg_h, uq_h, uk_h, udq_h, udk_h, nq_h, nk_h, ndq_h, ndk_h,
    osq_ref, osk_ref, osdq_ref, osdk_ref,
    tok, lq, lk, cq, ck, mq, mk, md, eq, ek, ed,
    wq, wk, wd, pq, pk, pd, yq, yk, yd, zq, zk, zd,
    normq, normk, turned, up, core_in, half, x_in, mine, pair_in, full,
    latent, gains, slope, tg, small, small_pair, small_z, small_row, small_core, small_lo, small_x,
    send_sems, recv_sems, local_sems,
):
    dp = lax.axis_index("dp")
    hd = lax.axis_index("head")
    yh, z = dp // NZ, dp % NZ
    x, yl, c = hd // 4, (hd // 2) % 2, hd % 2

    def z_dev(k):
        return (yh * NZ + (z + k + NZ) % NZ, hd)

    def x_dev(k):
        return (dp, ((x + k + NX) % NX) * 4 + yl * 2 + c)

    other_half = ((1 - yh) * NZ + z, hd)
    other_low = (dp, x * 4 + (1 - yl) * 2 + c)
    other_core = (dp, x * 4 + yl * 2 + 1 - c)
    z_next = (z_dev(1), z_dev(-1))
    x_next = (x_dev(1), x_dev(-1))

    ids = {}
    sent = []

    def remote(key, src, dst, dev):
        i = ids.setdefault(key, len(ids))
        return pltpu.make_async_remote_copy(
            src_ref=src, dst_ref=dst, send_sem=send_sems.at[i], recv_sem=recv_sems.at[i],
            device_id=dev, device_id_type=MESH,
        )

    def send(key, src, dst, dev):
        copy = remote(key, src, dst, dev)
        copy.start()
        sent.append(copy)

    def recv(key, land):
        remote(key, land, land, other_core).wait_recv()

    n_local = [0]

    def fetch(src, dst):
        copy = pltpu.make_async_copy(src, dst, local_sems.at[n_local[0]])
        n_local[0] += 1
        copy.start()
        return copy

    l_mk, l_mq = fetch(mk_h, mk), fetch(mq_h, mq)
    l_lk, l_ck = fetch(lk_h, lk), fetch(ck_h, ck)
    l_lq, l_cq = fetch(lq_h, lq), fetch(cq_h, cq)
    l_md = (fetch(mdq_h, md.at[pl.ds(0, QR)]), fetch(mdk_h, md.at[pl.ds(QR, KR)]))
    l_tok = fetch(tok_h, tok)
    l_eq, l_ek = fetch(eq_h, eq), fetch(ek_h, ek)
    l_ed = (fetch(edq_h, ed.at[pl.ds(0, QR)]), fetch(edk_h, ed.at[pl.ds(QR, KR)]))

    barrier = pltpu.get_barrier_semaphore()
    peers = [z_dev(k) for k in range(1, NZ)] + [x_dev(k) for k in range(1, NX)]
    peers += [other_half, other_low, other_core]
    for dev in peers:
        pl.semaphore_signal(barrier, inc=1, device_id=dev, device_id_type=MESH)

    def round_rows(src, dst, rows):
        def body(i):
            at = pl.ds(pl.multiple_of(i * 16, 16), 16)
            dst[at, :] = src[at, :].astype(bf16)

        loop(rows // 16, body)

    gathered = {"k": (wk, KR), "q": (wq, QR), "d": (wd, DR)}

    def gather_pair(w):
        ref, _ = gathered[w]
        send(("y", w), ref.at[place(0, 0)], ref.at[place(1, 0)], other_half)

    def gather_first(w, rel):
        ref, _ = gathered[w]
        if rel:
            recv(("y", w), ref.at[place(1, 0)])
        for side, sign in ((0, -1), (1, 1)):
            send(("g", w, rel, 1, side), ref.at[place(rel, 0)], ref.at[place(rel, sign)], z_next[side])

    def gather_next(w, rel, step):
        ref, rows = gathered[w]
        h = rows // 2
        for side, sign in ((0, -1), (1, 1)):
            here = ref.at[place(rel, sign * step)]
            if step == 4:
                recv(("g", w, rel, 4, side), here.at[pl.ds(side * h, h)])
                continue
            recv(("g", w, rel, step, side), here)
            there = ref.at[place(rel, sign * (step + 1))]
            if step == 3:
                here, there = here.at[pl.ds(side * h, h)], there.at[pl.ds(side * h, h)]
            send(("g", w, rel, step + 1, side), here, there, z_next[side])

    def own_block(ref, half_of, d):
        return ref.at[half_of * NZ + (z + d) % NZ]

    scattered = {
        "k": (lambda d: own_block(pk, yh, d), lambda d: own_block(pk, 1 - yh, d), yk, zk, KR),
        "q": (lambda d: own_block(pq, yh, d), lambda d: own_block(pq, 1 - yh, d), yq, zq, QR),
        "d": (lambda d: pd.at[place(0, d)], lambda d: pd.at[place(1, d)], yd, zd, DR),
    }

    def scatter_pair(w, d):
        _, theirs, y, _, _ = scattered[w]
        send(("sy", w, d), theirs(d), y.at[d], other_half)

    def scatter_first(w):
        own, _, y, zz, rows = scattered[w]
        h = rows // 2
        recv(("sy", w, 4), y.at[4])
        add_into([own(4), y.at[4]], own(4), 0, rows)
        for side in range(2):
            at = pl.ds(side * h, h)
            send(("s", w, 0, side), own(4).at[at], zz.at[side, 0].at[at], z_next[side])

    def scatter_next(w, step):
        own, _, y, zz, rows = scattered[w]
        h = rows // 2
        for side in range(2):
            d = 3 - step if side == 0 else 5 + step
            recv(("sy", w, d), y.at[d])
            if step == 0:
                came = zz.at[side, 0]
                recv(("s", w, 0, side), came.at[pl.ds(side * h, h)])
                add_into([own(d), y.at[d], came], own(d), side * h, h)
                add_into([own(d), y.at[d]], own(d), (1 - side) * h, h)
            else:
                came = zz.at[side, step]
                recv(("s", w, step, side), came)
                add_into([own(d), y.at[d], came], own(d), 0, rows)
            send(("s", w, step + 1, side), own(d), zz.at[side, step + 1], z_next[side])

    def scatter_last(w):
        own, _, y, zz, _ = scattered[w]
        recv(("sy", w, 0), y.at[0])
        recv(("s", w, 3, 0), zz.at[0, 3])
        recv(("s", w, 3, 1), zz.at[1, 3])
        return [own(0), y.at[0], zz.at[0, 3], zz.at[1, 3]]

    l_mk.wait()
    round_rows(mk, wk.at[place(0, 0)], KR)
    l_mq.wait()
    round_rows(mq, wq.at[place(0, 0)], QR)
    pl.semaphore_wait(barrier, len(peers))
    gather_pair("k")
    gather_first("k", 0)
    gather_pair("q")
    gather_first("q", 0)
    for load in l_md:
        load.wait()
    round_rows(md, wd.at[place(0, 0)], DR)

    def normalize(src, gain_ref, dst, width):
        def body(i):
            at = pl.ds(pl.multiple_of(i * 16, 16), 16)
            values = src[at, :].astype(f32)
            inverse = lax.rsqrt(jnp.sum(values * values, axis=1, keepdims=True) / width + norm_eps)
            dst[at, :] = (values * inverse * gain_ref[...]).astype(bf16)

        loop(TOK // 16, body)

    def turn(src, start, width):
        def body(i):
            at = pl.ds(pl.multiple_of(i * 128, 128), 128)
            block = src[at, pl.ds(start, width)]
            turned[pl.ds(0, width), at] = block.T

        loop(TOK // 128, body)

    def part_keyval(half_of):
        turn(normk, pl.multiple_of(half_of * 256, 128), 256)

        def body(i):
            at = pl.ds(pl.multiple_of(i * 512, 512), 512)
            out = dot(turned[pl.ds(0, 256), :], ck[:, at]).astype(bf16)
            pk[pl.ds(half_of * NZ, NZ), :, at] = out.reshape(NZ, KR, 512)

        loop(KC // 512, body)

    def part_query(half_of):
        def chunk(q):
            turn(normq, pl.multiple_of(half_of * 768 + q * GQ, 128), GQ)

            def body(i):
                at = pl.ds(pl.multiple_of(i * 512, 512), 512)
                out = dot(turned[pl.ds(0, GQ), :], cq[:, at]).astype(bf16)
                pq[pl.ds(half_of * NZ + q * 4, 4), :, at] = out.reshape(4, QR, 512)

            loop(QC // 512, body)

        loop(2, chunk)

    first_token = pl.multiple_of(c * (TOK // 2) + x * SLICE, 16)

    def arrange(src, gain_ref, rows, natural, width, group, at):
        lane = lax.broadcasted_iota(jnp.int32, (1, 4 * rows), 1)
        j = sum((lane >= rows * k).astype(jnp.int32) for k in (1, 2, 3))
        inside = lane - j * rows
        rel, back = j // 2, j % 2
        d = back * (NZ // 2) if group == 0 else jnp.where(back == 1, NZ - group, group)
        owner = jnp.where(rel == 1, 1 - yh, yh) * NZ + (z + d) % NZ
        source = owner * rows + inside
        chosen = (lax.broadcasted_iota(jnp.int32, (width, 4 * rows), 0) == source).astype(f32).astype(bf16)
        latent[group, :, at] = dot(src[pl.ds(first_token, SLICE), :], chosen)
        gain = jnp.broadcast_to(gain_ref[...], (8, width))
        gains[group, :, at] = select_dot(gain, chosen)

    def arrange_group(g):
        arrange(lq, gq_ref, QR, 0, QL, g, pl.ds(0, GQ))
        arrange(lk, gk_ref, KR, 0, KVL, g, pl.ds(GQ, GK))

    def upstream(g):
        def body(i):
            at = pl.ds(pl.multiple_of(i * 160, 160), 160)
            up[g, at, pl.ds(0, GQ)] = dot_t(cq[at, :], wq[g].reshape(GQ, QC)).astype(bf16)
            up[g, at, pl.ds(GQ, GK)] = dot_t(ck[at, :], wk[g].reshape(GK, KC)).astype(bf16)

        loop(TOK // 160, body)
        there = pl.ds(pl.multiple_of((1 - c) * 320, 16), 320)
        send(("c", g), up.at[g, there], core_in.at[g], other_core)

    def after_core(g):
        recv(("c", g), core_in.at[g])
        here = up.at[g, pl.ds(pl.multiple_of(c * 320, 16), 320)]
        add_into([here, core_in.at[g]], half.at[g], 0, 320)
        for k in (2, 1, 3):
            to = (x + k) % NX
            send(("x", g, k), half.at[g, pl.ds(pl.multiple_of(to * SLICE, 16), SLICE)], x_in.at[g, k - 1], x_dev(k))

    def after_x(g):
        for k in range(1, NX):
            recv(("x", g, k), x_in.at[g, k - 1])
        here = half.at[g, pl.ds(pl.multiple_of(x * SLICE, 16), SLICE)]
        add_into([here] + [x_in.at[g, k] for k in range(NX - 1)], mine.at[g], 0, SLICE)
        send(("l", g), mine.at[g], pair_in.at[g], other_low)

    def after_low(g):
        recv(("l", g), pair_in.at[g])
        add_into([mine.at[g], pair_in.at[g]], full.at[g], 0, SLICE)

    l_lk.wait()
    normalize(lk, gk_ref, normk, KVL)
    l_ck.wait()
    part_keyval(1 - yh)
    for d in (4, 3, 5):
        scatter_pair("k", d)
    gather_first("k", 1)
    l_lq.wait()
    normalize(lq, gq_ref, normq, QL)
    gather_first("q", 1)
    gather_next("k", 0, 1)
    gather_next("q", 0, 1)
    l_cq.wait()
    part_query(1 - yh)
    scatter_pair("q", 4)
    gather_next("k", 1, 1)
    gather_next("q", 1, 1)
    scatter_pair("q", 3)
    upstream(1)
    after_core(1)

    gather_next("k", 0, 2)
    part_keyval(yh)
    gather_next("q", 0, 2)
    scatter_pair("q", 5)
    gather_next("k", 1, 2)
    scatter_pair("k", 2)
    gather_next("q", 1, 2)
    after_x(1)
    scatter_pair("q", 2)
    upstream(2)
    after_core(2)

    gather_next("k", 0, 3)
    part_query(yh)
    gather_next("q", 0, 3)
    scatter_pair("k", 6)
    gather_next("k", 1, 3)
    scatter_pair("q", 6)
    arrange_group(0)
    arrange_group(1)
    gather_next("q", 1, 3)
    after_x(2)
    scatter_pair("q", 1)
    upstream(3)
    after_core(3)

    gather_next("k", 0, 4)
    gather_next("q", 0, 4)
    scatter_pair("k", 1)
    scatter_first("k")
    gather_next("k", 1, 4)
    scatter_first("q")
    after_low(1)
    gather_next("q", 1, 4)
    gather_first("d", 0)
    upstream(0)
    after_x(3)
    scatter_pair("k", 7)
    scatter_next("k", 0)
    after_core(0)
    scatter_next("q", 0)
    gather_next("d", 0, 1)
    after_x(0)
    scatter_pair("q", 7)
    scatter_pair("k", 0)
    gather_pair("d")
    scatter_pair("q", 0)
    arrange_group(2)
    arrange_group(3)
    scatter_next("k", 1)
    for g in (2, 3, 0):
        after_low(g)

    own_rows = pl.ds(first_token, SLICE)

    def norm_back(i):
        at = pl.ds(pl.multiple_of(i * 16, 16), 16)
        to = pl.ds(pl.multiple_of(first_token + i * 16, 16), 16)
        for first, width, units in ((0, GQ, QL), (GQ, GK, KVL)):
            cols = pl.ds(first, width)
            squares = 0.0
            inner = 0.0
            for g in range(4):
                values = latent[g, at, cols]
                squares += jnp.sum(values * values, axis=1, keepdims=True)
                inner += jnp.sum(values * gains[g, pl.ds(0, 1), cols] * full[g, at, cols], axis=1, keepdims=True)
            inverse = lax.rsqrt(squares / units + norm_eps)
            scale = inverse * inverse * inverse * (inner / units)
            for g in range(4):
                weighted = gains[g, pl.ds(0, 1), cols] * full[g, at, cols]
                slope[to, pl.ds(g * GW + first, width)] = (inverse * weighted - latent[g, at, cols] * scale).astype(bf16)

    loop(SLICE // 16, norm_back)

    sides = (pl.ds(0, 2 * GW), pl.ds(2 * GW, 2 * GW))

    def block_rows(k, core):
        return pl.ds(pl.multiple_of(core * 320 + ((x + k + NX) % NX) * SLICE, 16), SLICE)

    for part in range(2):
        for side in range(2):
            cols = sides[part if side == 0 else 1 - part]
            view = slope.at[own_rows, cols]
            send(("a", 1, side, part), view, view, x_next[side])
    view = slope.at[own_rows, :]
    send(("ac", 0), view, view, other_core)
    scatter_next("q", 1)
    for side, back in ((0, -1), (1, 1)):
        view = slope.at[block_rows(back, c), sides[side]]
        recv(("a", 1, side, 0), view)
        send(("a", 2, side), view, view, x_next[side])
    gather_next("d", 0, 2)
    scatter_next("k", 2)
    for side, back in ((0, -1), (1, 1)):
        recv(("a", 1, side, 1), slope.at[block_rows(back, c), sides[1 - side]])
        view = slope.at[block_rows(back, c), :]
        send(("ac", 1 + side), view, view, other_core)
    for side in range(2):
        recv(("a", 2, side), slope.at[block_rows(2, c), sides[side]])
    view = slope.at[block_rows(2, c), :]
    send(("ac", 3), view, view, other_core)
    scatter_next("q", 2)
    for i, k in enumerate((0, -1, 1, 2)):
        recv(("ac", i), slope.at[block_rows(k, 1 - c), :])

    l_tok.wait()
    for g in range(4):
        turn(slope, g * GW, GW)
        out = dot_t(turned[...], tok[...]).astype(bf16)
        pd[g, :, pl.ds(0, QR), :] = out[:GQ].reshape(4, QR, DC)
        pd[g, :, pl.ds(QR, KR), :] = out[GQ:].reshape(4, KR, DC)
    for d in (4, 3, 5, 2):
        scatter_pair("d", d)
    gather_next("d", 0, 3)

    def finish(refs, grad, mean, rows, cols):
        def step(i, squares):
            at = pl.ds(pl.multiple_of(i * 16, 16), 16)
            g = total(refs, at) / TOKENS
            mean[at, :] = beta_first * mean[at, :] + (1.0 - beta_first) * g
            return squares + g[0:8] * g[0:8] + g[8:16] * g[8:16]

        return lax.fori_loop(0, rows // 16, step, jnp.zeros((8, cols), f32))

    def heads_of(width, per_head):
        col = lax.broadcasted_iota(jnp.int32, (width, 128), 0)
        head = lax.broadcasted_iota(jnp.int32, (width, 128), 1)
        return ((col >= head * per_head) & (col < (head + 1) * per_head)).astype(f32).astype(bf16)

    def columns_of(width, per_head):
        head = lax.broadcasted_iota(jnp.int32, (128, width), 0)
        col = lax.broadcasted_iota(jnp.int32, (128, width), 1)
        return ((col >= head * per_head) & (col < (head + 1) * per_head)).astype(f32).astype(bf16)

    l_ek.wait()
    squares_k = finish(scatter_last("k"), None, ek, KR, KC)
    heads_k = jnp.sum(select_dot(squares_k, heads_of(KC, KVH)), axis=0, keepdims=True) / (KVL * KVH)
    scatter_first("d")
    gather_first("d", 1)
    l_eq.wait()
    squares_q = finish(scatter_last("q"), None, eq, QR, QC)
    heads_q = jnp.sum(select_dot(squares_q, heads_of(QC, QK)), axis=0, keepdims=True) / (QL * QK)
    row8 = lax.broadcasted_iota(jnp.int32, (8, 128), 0)
    small[...] = jnp.where(row8 == 0, heads_q, jnp.where(row8 == 1, heads_k, 0.0))
    send(("hy",), small, small_pair, other_half)
    for d in (6, 1, 7, 0):
        scatter_pair("d", d)
    scatter_next("d", 0)
    gather_next("d", 1, 1)
    recv(("hy",), small_pair)
    small_z[0] = small[...] + small_pair[...]
    for k in range(1, NZ):
        send(("hz", k), small_z.at[0], small_z.at[k], z_dev(k))
    gather_next("d", 0, 4)
    scatter_next("d", 1)
    gather_next("d", 1, 2)

    def token_grad(i):
        at = pl.ds(pl.multiple_of(i * 128, 128), 128)
        out = jnp.zeros((128, DC), f32)
        for g in range(4):
            out += dot(slope[at, pl.ds(g * GW, GQ)], wd[g, :, pl.ds(0, QR), :].reshape(GQ, DC))
            out += dot(slope[at, pl.ds(g * GW + GQ, GK)], wd[g, :, pl.ds(QR, KR), :].reshape(GK, DC))
        tg[:, at] = out.T.astype(bf16)

    for k in range(1, NZ):
        recv(("hz", k), small_z.at[k])
    heads = small_z[0]
    for k in range(1, NZ):
        heads = heads + small_z[k]
    small_row[...] = jnp.zeros((8, 128), f32)
    small_row[pl.ds(0, 1), pl.ds(0, 8)] = sq_ref[...]
    small_row[pl.ds(1, 1), pl.ds(0, 8)] = sk_ref[...]
    second = beta_second * small_row[...] + (1.0 - beta_second) * heads
    osq_ref[...] = second[0:1, 0:8]
    osk_ref[...] = second[1:2, 0:8]

    def update(second_wide, mean, out, rows):
        factor = 1.0 / (jnp.sqrt(second_wide / second_scale) + adam_eps)

        def body(i):
            at = pl.ds(pl.multiple_of(i * 16, 16), 16)
            out[at, :] = mean[at, :] / first_scale * factor

        loop(rows // 16, body)

    update(select_dot(second, columns_of(QC, QK))[0:1], eq, mq, QR)
    update(select_dot(second, columns_of(KC, KVH))[1:2], ek, mk, KR)
    stores = [fetch(eq, nq_h), fetch(ek, nk_h), fetch(mq, uq_h), fetch(mk, uk_h)]

    scatter_next("d", 2)
    gather_next("d", 1, 3)
    eye = lax.broadcasted_iota(jnp.int32, (128, 128), 0) == lax.broadcasted_iota(jnp.int32, (128, 128), 1)
    small_row[...] = jnp.zeros((8, 128), f32)
    small_row[pl.ds(0, 1), pl.ds(0, QR)] = sdq_ref[...]
    small_row[pl.ds(0, 1), pl.ds(QR, KR)] = sdk_ref[...]
    old = small_row[pl.ds(0, 1), :]
    for load in l_ed:
        load.wait()
    grad = total(scatter_last("d"), slice(None)) / TOKENS
    mean_next = beta_first * ed[...] + (1.0 - beta_first) * grad
    ed[...] = mean_next
    column = jnp.sum(grad * grad, axis=1, keepdims=True) / D
    row = jnp.sum(jnp.where(eye, column, 0.0), axis=0, keepdims=True)
    small_core[0] = jnp.broadcast_to(row, (8, 128))
    send(("rc",), small_core.at[0], small_core.at[1], other_core)
    stores += [fetch(ed.at[pl.ds(0, QR)], ndq_h), fetch(ed.at[pl.ds(QR, KR)], ndk_h)]
    gather_next("d", 1, 4)
    recv(("rc",), small_core.at[1])
    small_lo[0] = small_core[0] + small_core[1]
    send(("rl",), small_lo.at[0], small_lo.at[1], other_low)
    loop(TOK // 128, token_grad)
    stores += [fetch(tg, tg_h)]
    recv(("rl",), small_lo.at[1])
    small_x[0] = small_lo[0] + small_lo[1]
    for k in range(1, NX):
        send(("rx", k), small_x.at[0], small_x.at[k], x_dev(k))
    for k in range(1, NX):
        recv(("rx", k), small_x.at[k])
    rows_total = (small_x[0] + small_x[1]) + (small_x[2] + small_x[3])
    second_row = beta_second * old + (1.0 - beta_second) * rows_total[0:1]
    osdq_ref[...] = second_row[:, 0:QR]
    osdk_ref[...] = second_row[:, QR:DR]
    second_col = jnp.sum(jnp.where(eye, second_row, 0.0), axis=1, keepdims=True)
    factor = 1.0 / (jnp.sqrt(second_col / second_scale) + adam_eps)
    md[...] = mean_next / first_scale * factor
    stores += [fetch(md.at[pl.ds(0, QR)], udq_h), fetch(md.at[pl.ds(QR, KR)], udk_h)]

    for copy in sent:
        copy.wait_send()
    for store in stores:
        store.wait()


def publish(*refs):
    n = (len(refs) - 2) // 3
    into = [pltpu.make_async_copy(refs[i], refs[2 * n + i], refs[-2].at[i]) for i in range(n)]
    out = [pltpu.make_async_copy(refs[2 * n + i], refs[n + i], refs[-1].at[i]) for i in range(n)]
    for copy in into:
        copy.start()
    for i in range(n):
        into[i].wait()
        out[i].start()
    for copy in out:
        copy.wait()


def local(*args):
    (
        tokens, query_latent, keyval_latent, query_gain, keyval_gain, query_cotangent, keyval_cotangent,
        master_query_up, master_keyval_up, master_query_down, master_keyval_down,
        mean_query_up, mean_keyval_up, mean_query_down, mean_keyval_down,
        square_query_up, square_keyval_up, square_query_down, square_keyval_down,
    ) = args
    hbm = pl.BlockSpec(memory_space=pl.ANY)
    vmem = pl.BlockSpec(memory_space=pltpu.VMEM)

    def shape(rows, cols, kind=f32):
        return jax.ShapeDtypeStruct((rows, cols), kind)

    V = pltpu.VMEM
    outs = pl.pallas_call(
        kernel,
        name="backward_and_update",
        out_shape=(
            shape(DC, TOK, bf16),
            shape(QR, QC), shape(KR, KC), shape(QR, DC), shape(KR, DC),
            shape(QR, QC), shape(KR, KC), shape(QR, DC), shape(KR, DC),
            shape(1, 8), shape(1, 8), shape(1, QR), shape(1, KR),
        ),
        in_specs=[hbm] * 3 + [vmem] * 2 + [hbm] * 10 + [vmem] * 4,
        out_specs=(hbm,) * 9 + (vmem,) * 4,
        scratch_shapes=[
            V((DC, TOK), bf16), V((TOK, QL), bf16), V((TOK, KVL), bf16), V((TOK, QC), bf16), V((TOK, KC), bf16),
            V((QR, QC), f32), V((KR, KC), f32), V((DR, DC), f32),
            V((QR, QC), f32), V((KR, KC), f32), V((DR, DC), f32),
            V((4, 4, QR, QC), bf16), V((4, 4, KR, KC), bf16), V((4, 4, DR, DC), bf16),
            V((16, QR, QC), bf16), V((16, KR, KC), bf16), V((4, 4, DR, DC), bf16),
            V((8, QR, QC), bf16), V((8, KR, KC), bf16), V((8, DR, DC), bf16),
            V((2, 4, QR, QC), bf16), V((2, 4, KR, KC), bf16), V((2, 4, DR, DC), bf16),
            V((TOK, QL), bf16), V((TOK, KVL), bf16), V((GW, TOK), bf16),
            V((4, TOK, GW), bf16), V((4, 320, GW), bf16), V((4, 320, GW), bf16),
            V((4, 3, SLICE, GW), bf16), V((4, SLICE, GW), bf16), V((4, SLICE, GW), bf16), V((4, SLICE, GW), f32),
            V((4, SLICE, GW), f32), V((4, 8, GW), f32),
            V((TOK, 4 * GW), bf16), V((DC, TOK), bf16),
            V((8, 128), f32), V((8, 128), f32), V((8, 8, 128), f32), V((8, 128), f32),
            V((2, 8, 128), f32), V((2, 8, 128), f32), V((4, 8, 128), f32),
            pltpu.SemaphoreType.DMA((N_SEM,)), pltpu.SemaphoreType.DMA((N_SEM,)), pltpu.SemaphoreType.DMA((32,)),
        ],
        compiler_params=pltpu.CompilerParams(
            collective_id=0, has_side_effects=True, vmem_limit_bytes=62 * 2**20
        ),
        cost_estimate=pl.CostEstimate(flops=11 * 10**9, bytes_accessed=14 * 10**6, transcendentals=0),
    )(
        tokens.T, query_latent, keyval_latent, query_gain.reshape(1, QL), keyval_gain.reshape(1, KVL),
        query_cotangent, keyval_cotangent,
        master_query_up, master_keyval_up, master_query_down, master_keyval_down,
        mean_query_up, mean_keyval_up, mean_query_down, mean_keyval_down,
        square_query_up.reshape(1, 8), square_keyval_up.reshape(1, 8),
        square_query_down.reshape(1, QR), square_keyval_down.reshape(1, KR),
    )
    outs = pl.pallas_call(
        publish,
        name="publish",
        out_shape=tuple(jax.ShapeDtypeStruct(o.shape, o.dtype) for o in outs),
        in_specs=[hbm] * len(outs),
        out_specs=(hbm,) * len(outs),
        scratch_shapes=[V(o.shape, o.dtype) for o in outs]
        + [pltpu.SemaphoreType.DMA((len(outs),)), pltpu.SemaphoreType.DMA((len(outs),))],
    )(*outs)
    return (
        outs[0].T, *outs[1:9],
        outs[9].reshape(8), outs[10].reshape(8), outs[11].reshape(QR), outs[12].reshape(KR),
    )


def solution(mesh):
    both = P("dp", "head")
    return jax.shard_map(
        local,
        mesh=mesh,
        in_specs=(both, P("dp", None), P("dp", None), P(), P()) + (both,) * 10
        + (P("head"), P("head"), P("dp"), P("dp")),
        out_specs=(both,) * 9 + (P("head"), P("head"), P("dp"), P("dp")),
        check_vma=False,
    )
```

```python
import jax
import jax.numpy as jnp
from jax import lax
from jax.experimental import pallas as pl
from jax.experimental.pallas import tpu as pltpu
from jax.sharding import PartitionSpec as P

D = 7168
QL = 1536
KVL = 512
QK = 192
KVH = 256
TOKENS = 10240
TOK = 640

NZ = 8
NX = 4
DC = 448
QR, KR, DR = 96, 32, 448
GQ, GK, GW = 4 * QR, 4 * KR, 4 * (QR + KR)
QC, KC = 1536, 2048
DB = QR + KR
FAR = 128
SLICE = 80

norm_eps = 1e-06
adam_eps = 1e-08
beta_first = 0.9
beta_second = 0.95
adam_step = 10
first_scale = 1.0 - beta_first**adam_step
second_scale = 1.0 - beta_second**adam_step

MESH = pl.DeviceIdType.MESH
f32 = jnp.float32
bf16 = jnp.bfloat16
N_SEM = 192


def place(rel, d):
    d = d % NZ
    if d == 0 or d == NZ // 2:
        return (0, rel * 2 + (1 if d else 0))
    if d < NZ // 2:
        return (d, rel * 2)
    return (NZ - d, rel * 2 + 1)


def split3(a):
    hi = a.astype(bf16)
    rest = a - hi.astype(f32)
    mid = rest.astype(bf16)
    low = (rest - mid.astype(f32)).astype(bf16)
    return hi, mid, low


def dot(a, b):
    return jnp.dot(a, b, preferred_element_type=f32)


def dot_t(a, b):
    return lax.dot_general(a, b, (((1,), (1,)), ((), ())), preferred_element_type=f32)


def select_dot(a, chosen):
    hi, mid, low = split3(a)
    return dot(hi, chosen) + dot(mid, chosen) + dot(low, chosen)


def loop(count, body):
    def step(i, carry):
        body(i)
        return carry

    lax.fori_loop(0, count, step, 0)


def total(refs, rows):
    parts = [r[rows, :].astype(f32) for r in refs]
    out = parts[0]
    for p in parts[1:]:
        out = out + p
    return out


def add_into(refs, out, start, rows):
    def body(i):
        at = pl.ds(pl.multiple_of(start + i * 16, 16), 16)
        out[at, :] = total(refs, at).astype(out.dtype)

    loop(rows // 16, body)


def kernel(
    tok_h, lq_h, lk_h, gq_ref, gk_ref, cq_h, ck_h,
    mq_h, mk_h, mdq_h, mdk_h, eq_h, ek_h, edq_h, edk_h,
    sq_ref, sk_ref, sdq_ref, sdk_ref,
    tg_h, uq_h, uk_h, udq_h, udk_h, nq_h, nk_h, ndq_h, ndk_h,
    osq_ref, osk_ref, osdq_ref, osdk_ref,
    tok, lq, lk, cq, ck, mq, mk, md, eq, ek, ed,
    wq, wk, wd, pq, pk, pd, yq, yk, yd, zq, zk, zd,
    normq, normk, turned, up, core_in, half, x_in, mine, pair_in, full,
    latent, gains, by_block, raw, slope, tg, small, small_pair, small_z, small_row, small_core, small_x,
    gq_row, gk_row, send_sems, recv_sems, local_sems,
):
    dp = lax.axis_index("dp")
    hd = lax.axis_index("head")
    yh, z = dp // NZ, dp % NZ
    x, yl, c = hd // 4, (hd // 2) % 2, hd % 2

    def z_dev(k):
        return (yh * NZ + (z + k + NZ) % NZ, hd)

    def x_dev(k):
        return (dp, ((x + k + NX) % NX) * 4 + yl * 2 + c)

    def head_dev(k):
        low = 1 - yl if k >= NX else yl
        return (dp, ((x + k) % NX) * 4 + low * 2 + c)

    other_half = ((1 - yh) * NZ + z, hd)
    other_low = (dp, x * 4 + (1 - yl) * 2 + c)
    other_core = (dp, x * 4 + yl * 2 + 1 - c)
    z_next = (z_dev(1), z_dev(-1))
    x_next = (x_dev(1), x_dev(-1))

    ids = {}
    sent = []

    def remote(key, src, dst, dev):
        i = ids.setdefault(key, len(ids))
        return pltpu.make_async_remote_copy(
            src_ref=src, dst_ref=dst, send_sem=send_sems.at[i], recv_sem=recv_sems.at[i],
            device_id=dev, device_id_type=MESH,
        )

    def send(key, src, dst, dev):
        copy = remote(key, src, dst, dev)
        copy.start()
        sent.append(copy)

    def recv(key, land):
        remote(key, land, land, other_core).wait_recv()

    n_local = [0]

    def fetch(src, dst):
        copy = pltpu.make_async_copy(src, dst, local_sems.at[n_local[0]])
        n_local[0] += 1
        copy.start()
        return copy

    gq_row[...] = gq_ref[...].reshape(1, QL)
    gk_row[...] = gk_ref[...].reshape(1, KVL)
    l_mk, l_mq = fetch(mk_h, mk), fetch(mq_h, mq)
    l_lk, l_ck = fetch(lk_h, lk), fetch(ck_h, ck)
    l_lq, l_cq = fetch(lq_h, lq), fetch(cq_h, cq)
    l_md = (fetch(mdq_h, md.at[pl.ds(0, QR)]), fetch(mdk_h, md.at[pl.ds(QR, KR)]))
    l_tok = fetch(tok_h, tok)
    l_eq, l_ek = fetch(eq_h, eq), fetch(ek_h, ek)
    l_ed = (fetch(edq_h, ed.at[pl.ds(0, QR)]), fetch(edk_h, ed.at[pl.ds(QR, KR)]))

    barrier = pltpu.get_barrier_semaphore()
    peers = [z_dev(k) for k in range(1, NZ)] + [head_dev(k) for k in range(1, 2 * NX)]
    peers += [other_half, other_core]
    for dev in peers:
        pl.semaphore_signal(barrier, inc=1, device_id=dev, device_id_type=MESH)

    def round_rows(src, dst, rows):
        def body(i):
            at = pl.ds(pl.multiple_of(i * 16, 16), 16)
            dst[at, :] = src[at, :].astype(bf16)

        loop(rows // 16, body)

    gathered = {"k": (wk, KR), "q": (wq, QR), "d": (wd, DR)}

    def gather_pair(w):
        ref, _ = gathered[w]
        send(("y", w), ref.at[place(0, 0)], ref.at[place(1, 0)], other_half)

    def round_z(w, rel, ref):
        return ref.at[:, pl.ds(0, QC - FAR)] if w == "q" and rel else ref

    def gather_first(w, rel):
        ref, _ = gathered[w]
        if rel:
            recv(("y", w), ref.at[place(1, 0)])
        for side, sign in ((0, -1), (1, 1)):
            here, there = ref.at[place(rel, 0)], ref.at[place(rel, sign)]
            send(("g", w, rel, 1, side), round_z(w, rel, here), round_z(w, rel, there), z_next[side])

    def cross(d):
        far = pl.ds(QC - FAR, FAR)
        send(("b", d), wq.at[place(0, d)].at[:, far], wq.at[place(1, d)].at[:, far], other_half)

    def crossed(d):
        recv(("b", d), wq.at[place(1, d)].at[:, pl.ds(QC - FAR, FAR)])

    def gather_next(w, rel, step):
        ref, rows = gathered[w]
        h = rows // 2
        for side, sign in ((0, -1), (1, 1)):
            here = round_z(w, rel, ref.at[place(rel, sign * step)])
            if step == 4:
                recv(("g", w, rel, 4, side), here.at[pl.ds(side * h, h)])
                continue
            recv(("g", w, rel, step, side), here)
            there = round_z(w, rel, ref.at[place(rel, sign * (step + 1))])
            if step == 3:
                here, there = here.at[pl.ds(side * h, h)], there.at[pl.ds(side * h, h)]
            send(("g", w, rel, step + 1, side), here, there, z_next[side])
        if w == "q" and rel == 0 and step < 4:
            cross(step)
            cross(NZ - step)

    def far_half(d, side):
        return wq.at[place(1, d)].at[pl.ds(side * (QR // 2), QR // 2), pl.ds(QC - FAR, FAR)]

    def own_block(ref, half_of, d):
        return ref.at[half_of * NZ + (z + d) % NZ]

    scattered = {
        "k": (lambda d: own_block(pk, yh, d), lambda d: own_block(pk, 1 - yh, d), yk, zk, KR),
        "q": (lambda d: own_block(pq, yh, d), lambda d: own_block(pq, 1 - yh, d), yq, zq, QR),
        "d": (lambda d: pd.at[place(0, d)], lambda d: pd.at[place(1, d)], yd, zd, DR),
    }

    def scatter_pair(w, d):
        _, theirs, y, _, _ = scattered[w]
        send(("sy", w, d), theirs(d), y.at[d], other_half)

    def scatter_first(w):
        own, _, y, zz, rows = scattered[w]
        h = rows // 2
        recv(("sy", w, 4), y.at[4])
        add_into([own(4), y.at[4]], own(4), 0, rows)
        for side in range(2):
            at = pl.ds(side * h, h)
            send(("s", w, 0, side), own(4).at[at], zz.at[side, 0].at[at], z_next[side])

    def scatter_next(w, step):
        own, _, y, zz, rows = scattered[w]
        h = rows // 2
        for side in range(2):
            d = 3 - step if side == 0 else 5 + step
            recv(("sy", w, d), y.at[d])
            if step == 0:
                came = zz.at[side, 0]
                recv(("s", w, 0, side), came.at[pl.ds(side * h, h)])
                add_into([own(d), y.at[d], came], own(d), side * h, h)
                add_into([own(d), y.at[d]], own(d), (1 - side) * h, h)
            else:
                came = zz.at[side, step]
                recv(("s", w, step, side), came)
                add_into([own(d), y.at[d], came], own(d), 0, rows)
            send(("s", w, step + 1, side), own(d), zz.at[side, step + 1], z_next[side])

    def scatter_last(w):
        own, _, y, zz, _ = scattered[w]
        recv(("sy", w, 0), y.at[0])
        recv(("s", w, 3, 0), zz.at[0, 3])
        recv(("s", w, 3, 1), zz.at[1, 3])
        return [own(0), y.at[0], zz.at[0, 3], zz.at[1, 3]]

    l_mk.wait()
    round_rows(mk, wk.at[place(0, 0)], KR)
    l_mq.wait()
    round_rows(mq, wq.at[place(0, 0)], QR)
    pl.semaphore_wait(barrier, len(peers))
    gather_pair("k")
    gather_first("k", 0)
    gather_pair("q")
    gather_first("q", 0)
    for load in l_md:
        load.wait()
    wd[place(0, 0)] = md[...].T.astype(bf16)

    def normalize(src, gain_ref, dst, width):
        def body(i):
            at = pl.ds(pl.multiple_of(i * 32, 32), 32)
            values = src[at, :].astype(f32)
            inverse = lax.rsqrt(jnp.sum(values * values, axis=1, keepdims=True) / width + norm_eps)
            dst[at, :] = (values * inverse * gain_ref[...]).astype(bf16)

        loop(TOK // 32, body)

    def turn(src, start, width):
        def body(i):
            at = pl.ds(pl.multiple_of(i * 128, 128), 128)
            block = src[at, pl.ds(start, width)]
            turned[pl.ds(0, width), at] = block.T

        loop(TOK // 128, body)

    def part_keyval(half_of):
        turn(normk, pl.multiple_of(half_of * 256, 128), 256)

        def body(i):
            at = pl.ds(pl.multiple_of(i * 512, 512), 512)
            out = dot(turned[pl.ds(0, 256), :], ck[:, at]).astype(bf16)
            pk[pl.ds(half_of * NZ, NZ), :, at] = out.reshape(NZ, KR, 512)

        loop(KC // 512, body)

    def part_query(half_of):
        def chunk(q):
            turn(normq, pl.multiple_of(half_of * 768 + q * GQ, 128), GQ)

            def body(i):
                at = pl.ds(pl.multiple_of(i * 512, 512), 512)
                out = dot(turned[pl.ds(0, GQ), :], cq[:, at]).astype(bf16)
                pq[pl.ds(half_of * NZ + q * 4, 4), :, at] = out.reshape(4, QR, 512)

            loop(QC // 512, body)

        loop(2, chunk)

    first_token = pl.multiple_of(c * (TOK // 2) + x * SLICE, 16)

    def arrange(src, gain_ref, rows, natural, width, group, at):
        lane = lax.broadcasted_iota(jnp.int32, (1, 4 * rows), 1)
        j = sum((lane >= rows * k).astype(jnp.int32) for k in (1, 2, 3))
        inside = lane - j * rows
        rel, back = j // 2, j % 2
        d = back * (NZ // 2) if group == 0 else jnp.where(back == 1, NZ - group, group)
        owner = jnp.where(rel == 1, 1 - yh, yh) * NZ + (z + d) % NZ
        source = owner * rows + inside
        chosen = (lax.broadcasted_iota(jnp.int32, (width, 4 * rows), 0) == source).astype(f32).astype(bf16)
        latent[group, :, at] = dot(src[pl.ds(first_token, SLICE), :], chosen)
        gain = jnp.broadcast_to(gain_ref[...], (8, width))
        gains[group, :, at] = select_dot(gain, chosen)

    def arrange_blocks():
        col = lax.broadcasted_iota(jnp.int32, (1, GW), 1)
        j = sum((col >= DB * k).astype(jnp.int32) for k in (1, 2, 3))
        inside = col - j * DB
        source = jnp.where(inside < QR, j * QR + inside, GQ + j * KR + inside - QR)
        by_block[...] = (lax.broadcasted_iota(jnp.int32, (GW, GW), 0) == source).astype(f32).astype(bf16)

    def arrange_group(g):
        arrange(lq, gq_row, QR, 0, QL, g, pl.ds(0, GQ))
        arrange(lk, gk_row, KR, 0, KVL, g, pl.ds(GQ, GK))

    def upstream(g):
        if g:
            crossed(g)
            crossed(NZ - g)
        for side, d in ((0, -3), (1, 3)):
            if g == 3:
                send(("bf", side), far_half(d, side), far_half(4, side), z_next[side])
            if g == 0:
                recv(("bf", side), far_half(4, side))

        def body(i):
            at = pl.ds(pl.multiple_of(i * 160, 160), 160)
            up[g, at, pl.ds(0, GQ)] = dot_t(cq[at, :], wq[g].reshape(GQ, QC)).astype(bf16)
            up[g, at, pl.ds(GQ, GK)] = dot_t(ck[at, :], wk[g].reshape(GK, KC)).astype(bf16)

        loop(TOK // 160, body)
        there = pl.ds(pl.multiple_of((1 - c) * 320, 16), 320)
        send(("c", g), up.at[g, there], core_in.at[g], other_core)

    def after_core(g):
        recv(("c", g), core_in.at[g])
        here = up.at[g, pl.ds(pl.multiple_of(c * 320, 16), 320)]
        add_into([here, core_in.at[g]], half.at[g], 0, 320)
        for k in (2, 1, 3):
            to = (x + k) % NX
            send(("x", g, k), half.at[g, pl.ds(pl.multiple_of(to * SLICE, 16), SLICE)], x_in.at[g, k - 1], x_dev(k))

    def after_x(g):
        for k in range(1, NX):
            recv(("x", g, k), x_in.at[g, k - 1])
        here = half.at[g, pl.ds(pl.multiple_of(x * SLICE, 16), SLICE)]
        add_into([here] + [x_in.at[g, k] for k in range(NX - 1)], mine.at[g], 0, SLICE)
        send(("l", g), mine.at[g], pair_in.at[g], other_low)

    def after_low(g):
        recv(("l", g), pair_in.at[g])
        add_into([mine.at[g], pair_in.at[g]], full.at[g], 0, SLICE)

    l_lk.wait()
    normalize(lk, gk_row, normk, KVL)
    l_ck.wait()
    part_keyval(1 - yh)
    for d in (4, 3, 5):
        scatter_pair("k", d)
    gather_first("k", 1)
    l_lq.wait()
    normalize(lq, gq_row, normq, QL)
    gather_first("q", 1)
    gather_next("k", 0, 1)
    gather_next("q", 0, 1)
    l_cq.wait()
    part_query(1 - yh)
    scatter_pair("q", 4)
    gather_next("k", 1, 1)
    gather_next("q", 1, 1)
    scatter_pair("q", 3)
    upstream(1)

    gather_next("k", 0, 2)
    after_core(1)
    part_keyval(yh)
    gather_next("q", 0, 2)
    scatter_pair("q", 5)
    gather_next("k", 1, 2)
    scatter_pair("k", 2)
    gather_next("q", 1, 2)
    after_x(1)
    scatter_pair("q", 2)
    upstream(2)

    gather_next("k", 0, 3)
    after_core(2)
    part_query(yh)
    gather_next("q", 0, 3)
    scatter_pair("k", 6)
    gather_next("k", 1, 3)
    scatter_pair("q", 6)
    arrange_blocks()
    arrange_group(0)
    arrange_group(1)
    gather_next("q", 1, 3)
    after_x(2)
    scatter_pair("q", 1)
    upstream(3)

    gather_next("k", 0, 4)
    after_core(3)
    gather_next("q", 0, 4)
    scatter_first("k")
    gather_next("k", 1, 4)
    scatter_first("q")
    after_low(1)
    gather_next("q", 1, 4)
    gather_first("d", 0)
    upstream(0)
    after_x(3)
    scatter_next("k", 0)
    after_core(0)
    scatter_next("q", 0)
    gather_next("d", 0, 1)
    after_x(0)
    scatter_pair("k", 1)
    scatter_pair("k", 7)
    scatter_pair("q", 7)
    scatter_pair("k", 0)
    gather_pair("d")
    scatter_pair("q", 0)
    arrange_group(2)
    arrange_group(3)
    scatter_next("k", 1)
    for g in (2, 3, 0):
        after_low(g)

    own_rows = pl.ds(first_token, SLICE)

    def norm_back(i):
        at = pl.ds(pl.multiple_of(i * 16, 16), 16)
        for first, width, units in ((0, GQ, QL), (GQ, GK, KVL)):
            cols = pl.ds(first, width)
            squares = 0.0
            inner = 0.0
            for g in range(4):
                values = latent[g, at, cols]
                squares += jnp.sum(values * values, axis=1, keepdims=True)
                inner += jnp.sum(values * gains[g, pl.ds(0, 1), cols] * full[g, at, cols], axis=1, keepdims=True)
            inverse = lax.rsqrt(squares / units + norm_eps)
            scale = inverse * inverse * inverse * (inner / units)
            for g in range(4):
                weighted = gains[g, pl.ds(0, 1), cols] * full[g, at, cols]
                raw[at, pl.ds(g * GW + first, width)] = (inverse * weighted - latent[g, at, cols] * scale).astype(bf16)

    loop(SLICE // 16, norm_back)
    for g in range(4):
        cols = pl.ds(g * GW, GW)
        slope[own_rows, cols] = dot(raw[:, cols], by_block[...]).astype(bf16)

    sides = (pl.ds(0, 2 * GW), pl.ds(2 * GW, 2 * GW))

    def block_rows(k, core):
        return pl.ds(pl.multiple_of(core * 320 + ((x + k + NX) % NX) * SLICE, 16), SLICE)

    for part in range(2):
        for side in range(2):
            cols = sides[part if side == 0 else 1 - part]
            view = slope.at[own_rows, cols]
            send(("a", 1, side, part), view, view, x_next[side])
    view = slope.at[own_rows, :]
    send(("ac", 0), view, view, other_core)
    scatter_next("q", 1)
    for side, back in ((0, -1), (1, 1)):
        view = slope.at[block_rows(back, c), sides[side]]
        recv(("a", 1, side, 0), view)
        send(("a", 2, side), view, view, x_next[side])
    gather_next("d", 0, 2)
    scatter_next("k", 2)
    for side, back in ((0, -1), (1, 1)):
        recv(("a", 1, side, 1), slope.at[block_rows(back, c), sides[1 - side]])
        view = slope.at[block_rows(back, c), :]
        send(("ac", 1 + side), view, view, other_core)
    for side in range(2):
        recv(("a", 2, side), slope.at[block_rows(2, c), sides[side]])
    view = slope.at[block_rows(2, c), :]
    send(("ac", 3), view, view, other_core)
    scatter_next("q", 2)
    for i, k in enumerate((0, -1, 1, 2)):
        recv(("ac", i), slope.at[block_rows(k, 1 - c), :])

    l_tok.wait()
    for g, partners in ((0, (4,)), (3, (3, 5)), (2, (2,)), (1, ())):
        out = dot(tok[...], slope[:, pl.ds(g * GW, GW)]).astype(bf16)
        for j in range(4):
            pd[g, j] = out[:, j * DB : (j + 1) * DB]
        for d in partners:
            scatter_pair("d", d)
    gather_next("d", 0, 3)

    def finish(refs, grad, mean, rows, cols):
        def step(i, squares):
            at = pl.ds(pl.multiple_of(i * 16, 16), 16)
            g = total(refs, at) / TOKENS
            mean[at, :] = beta_first * mean[at, :] + (1.0 - beta_first) * g
            return squares + g[0:8] * g[0:8] + g[8:16] * g[8:16]

        return lax.fori_loop(0, rows // 16, step, jnp.zeros((8, cols), f32))

    def heads_of(width, per_head):
        col = lax.broadcasted_iota(jnp.int32, (width, 128), 0)
        head = lax.broadcasted_iota(jnp.int32, (width, 128), 1)
        return ((col >= head * per_head) & (col < (head + 1) * per_head)).astype(f32).astype(bf16)

    def columns_of(width, per_head):
        head = lax.broadcasted_iota(jnp.int32, (128, width), 0)
        col = lax.broadcasted_iota(jnp.int32, (128, width), 1)
        return ((col >= head * per_head) & (col < (head + 1) * per_head)).astype(f32).astype(bf16)

    l_ek.wait()
    squares_k = finish(scatter_last("k"), None, ek, KR, KC)
    heads_k = jnp.sum(select_dot(squares_k, heads_of(KC, KVH)), axis=0, keepdims=True) / (KVL * KVH)
    scatter_first("d")
    gather_first("d", 1)
    l_eq.wait()
    squares_q = finish(scatter_last("q"), None, eq, QR, QC)
    heads_q = jnp.sum(select_dot(squares_q, heads_of(QC, QK)), axis=0, keepdims=True) / (QL * QK)
    row8 = lax.broadcasted_iota(jnp.int32, (8, 128), 0)
    small[...] = jnp.where(row8 == 0, heads_q, jnp.where(row8 == 1, heads_k, 0.0))
    send(("hy",), small, small_pair, other_half)
    for d in (6, 1, 7, 0):
        scatter_pair("d", d)
    scatter_next("d", 0)
    gather_next("d", 1, 1)
    recv(("hy",), small_pair)
    small_z[0] = small[...] + small_pair[...]
    for k in range(1, NZ):
        send(("hz", k), small_z.at[0], small_z.at[k], z_dev(k))
    gather_next("d", 0, 4)
    scatter_next("d", 1)
    gather_next("d", 1, 2)

    def token_grad():
        out = jnp.zeros((DC, TOK), f32)
        for g in range(4):
            rows = jnp.concatenate([wd[g, j] for j in range(4)], axis=1)
            out += dot_t(rows, slope[:, pl.ds(g * GW, GW)])
        tg[...] = out.astype(bf16)

    for k in range(1, NZ):
        recv(("hz", k), small_z.at[k])
    heads = small_z[0]
    for k in range(1, NZ):
        heads = heads + small_z[k]
    small_row[...] = jnp.zeros((8, 128), f32)
    small_row[pl.ds(0, 1), pl.ds(0, 8)] = sq_ref[...]
    small_row[pl.ds(1, 1), pl.ds(0, 8)] = sk_ref[...]
    second = beta_second * small_row[...] + (1.0 - beta_second) * heads
    osq_ref[...] = second[0:1, 0:8]
    osk_ref[...] = second[1:2, 0:8]

    def update(second_wide, mean, out, rows):
        factor = 1.0 / (jnp.sqrt(second_wide / second_scale) + adam_eps)

        def body(i):
            at = pl.ds(pl.multiple_of(i * 16, 16), 16)
            out[at, :] = mean[at, :] / first_scale * factor

        loop(rows // 16, body)

    update(select_dot(second, columns_of(QC, QK))[0:1], eq, mq, QR)
    update(select_dot(second, columns_of(KC, KVH))[1:2], ek, mk, KR)
    stores = [fetch(eq, nq_h), fetch(ek, nk_h), fetch(mq, uq_h), fetch(mk, uk_h)]

    scatter_next("d", 2)
    gather_next("d", 1, 3)
    eye = lax.broadcasted_iota(jnp.int32, (128, 128), 0) == lax.broadcasted_iota(jnp.int32, (128, 128), 1)
    small_row[...] = jnp.zeros((8, 128), f32)
    small_row[pl.ds(0, 1), pl.ds(0, QR)] = sdq_ref[...]
    small_row[pl.ds(0, 1), pl.ds(QR, KR)] = sdk_ref[...]
    old = small_row[pl.ds(0, 1), :]
    for load in l_ed:
        load.wait()
    grad = total(scatter_last("d"), slice(None)).T / TOKENS
    mean_next = beta_first * ed[...] + (1.0 - beta_first) * grad
    ed[...] = mean_next
    column = jnp.sum(grad * grad, axis=1, keepdims=True) / D
    row = jnp.sum(jnp.where(eye, column, 0.0), axis=0, keepdims=True)
    small_core[0] = jnp.broadcast_to(row, (8, 128))
    send(("rc",), small_core.at[0], small_core.at[1], other_core)
    stores += [fetch(ed.at[pl.ds(0, QR)], ndq_h), fetch(ed.at[pl.ds(QR, KR)], ndk_h)]
    gather_next("d", 1, 4)
    recv(("rc",), small_core.at[1])
    small_x[0] = small_core[0] + small_core[1]
    for k in range(1, 2 * NX):
        send(("rx", k), small_x.at[0], small_x.at[k], head_dev(k))
    token_grad()
    stores += [fetch(tg, tg_h)]
    for k in range(1, 2 * NX):
        recv(("rx", k), small_x.at[k])
    rows_total = small_x[0]
    for k in range(1, 2 * NX):
        rows_total = rows_total + small_x[k]
    second_row = beta_second * old + (1.0 - beta_second) * rows_total[0:1]
    osdq_ref[...] = second_row[:, 0:QR]
    osdk_ref[...] = second_row[:, QR:DB]
    second_col = jnp.sum(jnp.where(eye, second_row, 0.0), axis=1, keepdims=True)
    factor = 1.0 / (jnp.sqrt(second_col / second_scale) + adam_eps)
    md[...] = mean_next / first_scale * factor
    stores += [fetch(md.at[pl.ds(0, QR)], udq_h), fetch(md.at[pl.ds(QR, KR)], udk_h)]

    for copy in sent:
        copy.wait_send()
    for store in stores:
        store.wait()


def publish(*refs):
    n = (len(refs) - 2) // 3
    into = [pltpu.make_async_copy(refs[i], refs[2 * n + i], refs[-2].at[i]) for i in range(n)]
    out = [pltpu.make_async_copy(refs[2 * n + i], refs[n + i], refs[-1].at[i]) for i in range(n)]
    for copy in into:
        copy.start()
    for i in range(n):
        into[i].wait()
        out[i].start()
    for copy in out:
        copy.wait()


def local(*args):
    (
        tokens, query_latent, keyval_latent, query_gain, keyval_gain, query_cotangent, keyval_cotangent,
        master_query_up, master_keyval_up, master_query_down, master_keyval_down,
        mean_query_up, mean_keyval_up, mean_query_down, mean_keyval_down,
        square_query_up, square_keyval_up, square_query_down, square_keyval_down,
    ) = args
    hbm = pl.BlockSpec(memory_space=pl.ANY)
    vmem = pl.BlockSpec(memory_space=pltpu.VMEM)

    def shape(rows, cols, kind=f32):
        return jax.ShapeDtypeStruct((rows, cols), kind)

    V = pltpu.VMEM
    outs = pl.pallas_call(
        kernel,
        name="backward_and_update",
        out_shape=(
            shape(DC, TOK, bf16),
            shape(QR, QC), shape(KR, KC), shape(QR, DC), shape(KR, DC),
            shape(QR, QC), shape(KR, KC), shape(QR, DC), shape(KR, DC),
            shape(1, 8), shape(1, 8), shape(1, QR), shape(1, KR),
        ),
        in_specs=[hbm] * 3 + [vmem] * 2 + [hbm] * 10 + [vmem] * 4,
        out_specs=(hbm,) * 9 + (vmem,) * 4,
        scratch_shapes=[
            V((DC, TOK), bf16), V((TOK, QL), bf16), V((TOK, KVL), bf16), V((TOK, QC), bf16), V((TOK, KC), bf16),
            V((QR, QC), f32), V((KR, KC), f32), V((DB, DC), f32),
            V((QR, QC), f32), V((KR, KC), f32), V((DB, DC), f32),
            V((4, 4, QR, QC), bf16), V((4, 4, KR, KC), bf16), V((4, 4, DC, DB), bf16),
            V((16, QR, QC), bf16), V((16, KR, KC), bf16), V((4, 4, DC, DB), bf16),
            V((8, QR, QC), bf16), V((8, KR, KC), bf16), V((8, DC, DB), bf16),
            V((2, 4, QR, QC), bf16), V((2, 4, KR, KC), bf16), V((2, 4, DC, DB), bf16),
            V((TOK, QL), bf16), V((TOK, KVL), bf16), V((GW, TOK), bf16),
            V((4, TOK, GW), bf16), V((4, 320, GW), bf16), V((4, 320, GW), bf16),
            V((4, 3, SLICE, GW), bf16), V((4, SLICE, GW), bf16), V((4, SLICE, GW), bf16), V((4, SLICE, GW), f32),
            V((4, SLICE, GW), f32), V((4, 8, GW), f32), V((GW, GW), bf16), V((SLICE, 4 * GW), bf16),
            V((TOK, 4 * GW), bf16), V((DC, TOK), bf16),
            V((8, 128), f32), V((8, 128), f32), V((8, 8, 128), f32), V((8, 128), f32),
            V((2, 8, 128), f32), V((8, 8, 128), f32),
            V((1, QL), f32), V((1, KVL), f32),
            pltpu.SemaphoreType.DMA((N_SEM,)), pltpu.SemaphoreType.DMA((N_SEM,)), pltpu.SemaphoreType.DMA((32,)),
        ],
        compiler_params=pltpu.CompilerParams(
            collective_id=0, has_side_effects=True, vmem_limit_bytes=62 * 2**20
        ),
        cost_estimate=pl.CostEstimate(flops=11 * 10**9, bytes_accessed=14 * 10**6, transcendentals=0),
    )(
        tokens.T, query_latent, keyval_latent, query_gain, keyval_gain,
        query_cotangent, keyval_cotangent,
        master_query_up, master_keyval_up, master_query_down, master_keyval_down,
        mean_query_up, mean_keyval_up, mean_query_down, mean_keyval_down,
        square_query_up.reshape(1, 8), square_keyval_up.reshape(1, 8),
        square_query_down.reshape(1, QR), square_keyval_down.reshape(1, KR),
    )
    outs = pl.pallas_call(
        publish,
        name="publish",
        out_shape=tuple(jax.ShapeDtypeStruct(o.shape, o.dtype) for o in outs),
        in_specs=[hbm] * len(outs),
        out_specs=(hbm,) * len(outs),
        scratch_shapes=[V(o.shape, o.dtype) for o in outs]
        + [pltpu.SemaphoreType.DMA((len(outs),)), pltpu.SemaphoreType.DMA((len(outs),))],
    )(*outs)
    return (
        outs[0].T, *outs[1:9],
        outs[9].reshape(8), outs[10].reshape(8), outs[11].reshape(QR), outs[12].reshape(KR),
    )


def solution(mesh):
    both = P("dp", "head")
    return jax.shard_map(
        local,
        mesh=mesh,
        in_specs=(both, P("dp", None), P("dp", None), P(), P()) + (both,) * 10
        + (P("head"), P("head"), P("dp"), P("dp")),
        out_specs=(both,) * 9 + (P("head"), P("head"), P("dp"), P("dp")),
        check_vma=False,
    )
```

```python
import jax
import jax.numpy as jnp
from jax import lax
from jax.experimental import pallas as pl
from jax.experimental.pallas import tpu as pltpu
from jax.sharding import PartitionSpec as P

D = 7168
QL = 1536
KVL = 512
QK = 192
KVH = 256
TOKENS = 10240
TOK = 640

NZ = 8
NX = 4
DC = 448
QR, KR, DR = 96, 32, 448
GQ, GK, GW = 4 * QR, 4 * KR, 4 * (QR + KR)
QC, KC = 1536, 2048
DB = QR + KR
FAR = 256
SLICE = 80

norm_eps = 1e-06
adam_eps = 1e-08
beta_first = 0.9
beta_second = 0.95
adam_step = 10
first_scale = 1.0 - beta_first**adam_step
second_scale = 1.0 - beta_second**adam_step

MESH = pl.DeviceIdType.MESH
f32 = jnp.float32
bf16 = jnp.bfloat16
N_SEM = 192


def place(rel, d):
    d = d % NZ
    if d == 0 or d == NZ // 2:
        return (0, rel * 2 + (1 if d else 0))
    if d < NZ // 2:
        return (d, rel * 2)
    return (NZ - d, rel * 2 + 1)


def split3(a):
    hi = a.astype(bf16)
    rest = a - hi.astype(f32)
    mid = rest.astype(bf16)
    low = (rest - mid.astype(f32)).astype(bf16)
    return hi, mid, low


def dot(a, b):
    return jnp.dot(a, b, preferred_element_type=f32)


def dot_t(a, b):
    return lax.dot_general(a, b, (((1,), (1,)), ((), ())), preferred_element_type=f32)


def select_dot(a, chosen):
    hi, mid, low = split3(a)
    return dot(hi, chosen) + dot(mid, chosen) + dot(low, chosen)


def loop(count, body):
    def step(i, carry):
        body(i)
        return carry

    lax.fori_loop(0, count, step, 0)


def total(refs, rows):
    parts = [r[rows, :].astype(f32) for r in refs]
    out = parts[0]
    for p in parts[1:]:
        out = out + p
    return out


def add_into(refs, out, start, rows):
    def body(i):
        at = pl.ds(pl.multiple_of(start + i * 16, 16), 16)
        out[at, :] = total(refs, at).astype(out.dtype)

    loop(rows // 16, body)


def kernel(
    tok_h, lq_h, lk_h, gq_ref, gk_ref, cq_h, ck_h,
    mq_h, mk_h, mdq_h, mdk_h, eq_h, ek_h, edq_h, edk_h,
    sq_ref, sk_ref, sdq_ref, sdk_ref,
    tg_h, uq_h, uk_h, udq_h, udk_h, nq_h, nk_h, ndq_h, ndk_h,
    osq_ref, osk_ref, osdq_ref, osdk_ref,
    tok, lq, lk, cq, ck, mq, mk, md, eq, ek, ed,
    wq, wk, wd, pq, pk, pd, yq, yk, yd, zq, zk, zd,
    normq, normk, turned, up, core_in, half, x_in, mine, pair_in, full,
    latent, gains, by_block, raw, slope, tg, small, small_pair, small_z, small_row, small_core, small_x,
    gq_row, gk_row, send_sems, recv_sems, local_sems,
):
    dp = lax.axis_index("dp")
    hd = lax.axis_index("head")
    yh, z = dp // NZ, dp % NZ
    x, yl, c = hd // 4, (hd // 2) % 2, hd % 2

    def z_dev(k):
        return (yh * NZ + (z + k + NZ) % NZ, hd)

    def x_dev(k):
        return (dp, ((x + k + NX) % NX) * 4 + yl * 2 + c)

    def head_dev(k):
        low = 1 - yl if k >= NX else yl
        return (dp, ((x + k) % NX) * 4 + low * 2 + c)

    other_half = ((1 - yh) * NZ + z, hd)
    other_low = (dp, x * 4 + (1 - yl) * 2 + c)
    other_core = (dp, x * 4 + yl * 2 + 1 - c)
    z_next = (z_dev(1), z_dev(-1))
    x_next = (x_dev(1), x_dev(-1))

    ids = {}
    sent = []

    def remote(key, src, dst, dev):
        i = ids.setdefault(key, len(ids))
        return pltpu.make_async_remote_copy(
            src_ref=src, dst_ref=dst, send_sem=send_sems.at[i], recv_sem=recv_sems.at[i],
            device_id=dev, device_id_type=MESH,
        )

    def send(key, src, dst, dev):
        copy = remote(key, src, dst, dev)
        copy.start()
        sent.append(copy)

    def recv(key, land):
        remote(key, land, land, other_core).wait_recv()

    n_local = [0]

    def fetch(src, dst):
        copy = pltpu.make_async_copy(src, dst, local_sems.at[n_local[0]])
        n_local[0] += 1
        copy.start()
        return copy

    gq_row[...] = gq_ref[...].reshape(1, QL)
    gk_row[...] = gk_ref[...].reshape(1, KVL)
    l_mk, l_mq = fetch(mk_h, mk), fetch(mq_h, mq)
    l_lk, l_ck = fetch(lk_h, lk), fetch(ck_h, ck)
    l_lq, l_cq = fetch(lq_h, lq), fetch(cq_h, cq)
    l_md = (fetch(mdq_h, md.at[pl.ds(0, QR)]), fetch(mdk_h, md.at[pl.ds(QR, KR)]))
    l_tok = fetch(tok_h, tok)
    l_eq, l_ek = fetch(eq_h, eq), fetch(ek_h, ek)
    l_ed = (fetch(edq_h, ed.at[pl.ds(0, QR)]), fetch(edk_h, ed.at[pl.ds(QR, KR)]))

    barrier = pltpu.get_barrier_semaphore()
    peers = [z_dev(k) for k in range(1, NZ)] + [head_dev(k) for k in range(1, 2 * NX)]
    peers += [other_half, other_core]
    for dev in peers:
        pl.semaphore_signal(barrier, inc=1, device_id=dev, device_id_type=MESH)

    def round_rows(src, dst, rows):
        def body(i):
            at = pl.ds(pl.multiple_of(i * 16, 16), 16)
            dst[at, :] = src[at, :].astype(bf16)

        loop(rows // 16, body)

    gathered = {"k": (wk, KR), "q": (wq, QR), "d": (wd, DR)}

    def gather_pair(w):
        ref, _ = gathered[w]
        send(("y", w), ref.at[place(0, 0)], ref.at[place(1, 0)], other_half)

    def round_z(w, rel, ref):
        return ref.at[:, pl.ds(0, QC - FAR)] if w == "q" and rel else ref

    def gather_first(w, rel):
        ref, _ = gathered[w]
        if rel:
            recv(("y", w), ref.at[place(1, 0)])
        for side, sign in ((0, -1), (1, 1)):
            here, there = ref.at[place(rel, 0)], ref.at[place(rel, sign)]
            send(("g", w, rel, 1, side), round_z(w, rel, here), round_z(w, rel, there), z_next[side])

    def cross(d):
        far = pl.ds(QC - FAR, FAR)
        send(("b", d), wq.at[place(0, d)].at[:, far], wq.at[place(1, d)].at[:, far], other_half)

    def crossed(d):
        recv(("b", d), wq.at[place(1, d)].at[:, pl.ds(QC - FAR, FAR)])

    def gather_next(w, rel, step):
        ref, rows = gathered[w]
        h = rows // 2
        for side, sign in ((0, -1), (1, 1)):
            here = round_z(w, rel, ref.at[place(rel, sign * step)])
            if step == 4:
                recv(("g", w, rel, 4, side), here.at[pl.ds(side * h, h)])
                continue
            recv(("g", w, rel, step, side), here)
            there = round_z(w, rel, ref.at[place(rel, sign * (step + 1))])
            if step == 3:
                here, there = here.at[pl.ds(side * h, h)], there.at[pl.ds(side * h, h)]
            send(("g", w, rel, step + 1, side), here, there, z_next[side])
        if w == "q" and rel == 0 and step < 4:
            cross(step)
            cross(NZ - step)

    def far_half(d, side):
        return wq.at[place(1, d)].at[pl.ds(side * (QR // 2), QR // 2), pl.ds(QC - FAR, FAR)]

    def own_block(ref, half_of, d):
        return ref.at[half_of * NZ + (z + d) % NZ]

    scattered = {
        "k": (lambda d: own_block(pk, yh, d), lambda d: own_block(pk, 1 - yh, d), yk, zk, KR),
        "q": (lambda d: own_block(pq, yh, d), lambda d: own_block(pq, 1 - yh, d), yq, zq, QR),
        "d": (lambda d: pd.at[place(0, d)], lambda d: pd.at[place(1, d)], yd, zd, DR),
    }

    def scatter_pair(w, d):
        _, theirs, y, _, _ = scattered[w]
        send(("sy", w, d), theirs(d), y.at[d], other_half)

    def scatter_first(w):
        own, _, y, zz, rows = scattered[w]
        h = rows // 2
        recv(("sy", w, 4), y.at[4])
        add_into([own(4), y.at[4]], own(4), 0, rows)
        for side in range(2):
            at = pl.ds(side * h, h)
            send(("s", w, 0, side), own(4).at[at], zz.at[side, 0].at[at], z_next[side])

    def scatter_next(w, step):
        own, _, y, zz, rows = scattered[w]
        h = rows // 2
        for side in range(2):
            d = 3 - step if side == 0 else 5 + step
            recv(("sy", w, d), y.at[d])
            if step == 0:
                came = zz.at[side, 0]
                recv(("s", w, 0, side), came.at[pl.ds(side * h, h)])
                add_into([own(d), y.at[d], came], own(d), side * h, h)
                add_into([own(d), y.at[d]], own(d), (1 - side) * h, h)
            else:
                came = zz.at[side, step]
                recv(("s", w, step, side), came)
                add_into([own(d), y.at[d], came], own(d), 0, rows)
            send(("s", w, step + 1, side), own(d), zz.at[side, step + 1], z_next[side])

    def scatter_last(w):
        own, _, y, zz, _ = scattered[w]
        recv(("sy", w, 0), y.at[0])
        recv(("s", w, 3, 0), zz.at[0, 3])
        recv(("s", w, 3, 1), zz.at[1, 3])
        return [own(0), y.at[0], zz.at[0, 3], zz.at[1, 3]]

    l_mk.wait()
    round_rows(mk, wk.at[place(0, 0)], KR)
    l_mq.wait()
    round_rows(mq, wq.at[place(0, 0)], QR)
    pl.semaphore_wait(barrier, len(peers))
    gather_pair("k")
    gather_first("k", 0)
    gather_pair("q")
    gather_first("q", 0)
    for load in l_md:
        load.wait()
    wd[place(0, 0)] = md[...].T.astype(bf16)

    def normalize(src, gain_ref, dst, width):
        def body(i):
            at = pl.ds(pl.multiple_of(i * 32, 32), 32)
            values = src[at, :].astype(f32)
            inverse = lax.rsqrt(jnp.sum(values * values, axis=1, keepdims=True) / width + norm_eps)
            dst[at, :] = (values * inverse * gain_ref[...]).astype(bf16)

        loop(TOK // 32, body)

    def turn(src, start, width):
        def body(i):
            at = pl.ds(pl.multiple_of(i * 128, 128), 128)
            block = src[at, pl.ds(start, width)]
            turned[pl.ds(0, width), at] = block.T

        loop(TOK // 128, body)

    def part_keyval(half_of):
        turn(normk, pl.multiple_of(half_of * 256, 128), 256)

        def body(i):
            at = pl.ds(pl.multiple_of(i * 512, 512), 512)
            out = dot(turned[pl.ds(0, 256), :], ck[:, at]).astype(bf16)
            pk[pl.ds(half_of * NZ, NZ), :, at] = out.reshape(NZ, KR, 512)

        loop(KC // 512, body)

    def part_query(half_of):
        def chunk(q):
            turn(normq, pl.multiple_of(half_of * 768 + q * GQ, 128), GQ)

            def body(i):
                at = pl.ds(pl.multiple_of(i * 512, 512), 512)
                out = dot(turned[pl.ds(0, GQ), :], cq[:, at]).astype(bf16)
                pq[pl.ds(half_of * NZ + q * 4, 4), :, at] = out.reshape(4, QR, 512)

            loop(QC // 512, body)

        loop(2, chunk)

    first_token = pl.multiple_of(c * (TOK // 2) + x * SLICE, 16)

    def arrange(src, gain_ref, rows, natural, width, group, at):
        lane = lax.broadcasted_iota(jnp.int32, (1, 4 * rows), 1)
        j = sum((lane >= rows * k).astype(jnp.int32) for k in (1, 2, 3))
        inside = lane - j * rows
        rel, back = j // 2, j % 2
        d = back * (NZ // 2) if group == 0 else jnp.where(back == 1, NZ - group, group)
        owner = jnp.where(rel == 1, 1 - yh, yh) * NZ + (z + d) % NZ
        source = owner * rows + inside
        chosen = (lax.broadcasted_iota(jnp.int32, (width, 4 * rows), 0) == source).astype(f32).astype(bf16)
        latent[group, :, at] = dot(src[pl.ds(first_token, SLICE), :], chosen)
        gain = jnp.broadcast_to(gain_ref[...], (8, width))
        gains[group, :, at] = select_dot(gain, chosen)

    def arrange_blocks():
        col = lax.broadcasted_iota(jnp.int32, (1, GW), 1)
        j = sum((col >= DB * k).astype(jnp.int32) for k in (1, 2, 3))
        inside = col - j * DB
        source = jnp.where(inside < QR, j * QR + inside, GQ + j * KR + inside - QR)
        by_block[...] = (lax.broadcasted_iota(jnp.int32, (GW, GW), 0) == source).astype(f32).astype(bf16)

    def arrange_group(g):
        arrange(lq, gq_row, QR, 0, QL, g, pl.ds(0, GQ))
        arrange(lk, gk_row, KR, 0, KVL, g, pl.ds(GQ, GK))

    def upstream(g):
        if g:
            crossed(g)
            crossed(NZ - g)
        for side, d in ((0, -3), (1, 3)):
            if g == 3:
                send(("bf", side), far_half(d, side), far_half(4, side), z_next[side])
            if g == 0:
                recv(("bf", side), far_half(4, side))

        def body(i):
            at = pl.ds(pl.multiple_of(i * 320, 320), 320)
            up[g, at, pl.ds(0, GQ)] = dot_t(cq[at, :], wq[g].reshape(GQ, QC)).astype(bf16)
            up[g, at, pl.ds(GQ, GK)] = dot_t(ck[at, :], wk[g].reshape(GK, KC)).astype(bf16)

        loop(TOK // 320, body)
        there = pl.ds(pl.multiple_of((1 - c) * 320, 16), 320)
        send(("c", g), up.at[g, there], core_in.at[g], other_core)

    def after_core(g):
        recv(("c", g), core_in.at[g])
        here = up.at[g, pl.ds(pl.multiple_of(c * 320, 16), 320)]
        add_into([here, core_in.at[g]], half.at[g], 0, 320)
        for k in (2, 1, 3):
            to = (x + k) % NX
            send(("x", g, k), half.at[g, pl.ds(pl.multiple_of(to * SLICE, 16), SLICE)], x_in.at[g, k - 1], x_dev(k))

    def after_x(g):
        for k in range(1, NX):
            recv(("x", g, k), x_in.at[g, k - 1])
        here = half.at[g, pl.ds(pl.multiple_of(x * SLICE, 16), SLICE)]
        add_into([here] + [x_in.at[g, k] for k in range(NX - 1)], mine.at[g], 0, SLICE)
        send(("l", g), mine.at[g], pair_in.at[g], other_low)

    def after_low(g):
        recv(("l", g), pair_in.at[g])
        add_into([mine.at[g], pair_in.at[g]], full.at[g], 0, SLICE)

    l_lk.wait()
    normalize(lk, gk_row, normk, KVL)
    l_ck.wait()
    part_keyval(1 - yh)
    for d in (4, 3, 5):
        scatter_pair("k", d)
    gather_first("k", 1)
    l_lq.wait()
    normalize(lq, gq_row, normq, QL)
    gather_first("q", 1)
    gather_next("k", 0, 1)
    gather_next("q", 0, 1)
    l_cq.wait()
    part_query(1 - yh)
    scatter_pair("q", 4)
    gather_next("k", 1, 1)
    gather_next("q", 1, 1)
    scatter_pair("q", 3)
    upstream(1)

    gather_next("k", 0, 2)
    after_core(1)
    part_keyval(yh)
    gather_next("q", 0, 2)
    scatter_pair("q", 5)
    gather_next("k", 1, 2)
    scatter_pair("k", 2)
    gather_next("q", 1, 2)
    after_x(1)
    scatter_pair("q", 2)
    upstream(2)

    gather_next("k", 0, 3)
    after_core(2)
    part_query(yh)
    gather_next("q", 0, 3)
    scatter_pair("k", 6)
    gather_next("k", 1, 3)
    scatter_pair("q", 6)
    arrange_blocks()
    arrange_group(0)
    arrange_group(1)
    gather_next("q", 1, 3)
    after_x(2)
    scatter_pair("q", 1)
    upstream(3)

    gather_next("k", 0, 4)
    after_core(3)
    gather_next("q", 0, 4)
    scatter_first("k")
    gather_next("k", 1, 4)
    scatter_first("q")
    after_low(1)
    gather_next("q", 1, 4)
    gather_first("d", 0)
    upstream(0)
    after_x(3)
    scatter_next("k", 0)
    after_core(0)
    scatter_next("q", 0)
    gather_next("d", 0, 1)
    after_x(0)
    scatter_pair("k", 1)
    scatter_pair("k", 7)
    scatter_pair("q", 7)
    scatter_pair("k", 0)
    gather_pair("d")
    scatter_pair("q", 0)
    arrange_group(2)
    arrange_group(3)
    scatter_next("k", 1)
    for g in (2, 3, 0):
        after_low(g)

    own_rows = pl.ds(first_token, SLICE)

    def norm_back(i):
        at = pl.ds(pl.multiple_of(i * 16, 16), 16)
        for first, width, units in ((0, GQ, QL), (GQ, GK, KVL)):
            cols = pl.ds(first, width)
            squares = 0.0
            inner = 0.0
            for g in range(4):
                values = latent[g, at, cols]
                squares += jnp.sum(values * values, axis=1, keepdims=True)
                inner += jnp.sum(values * gains[g, pl.ds(0, 1), cols] * full[g, at, cols], axis=1, keepdims=True)
            inverse = lax.rsqrt(squares / units + norm_eps)
            scale = inverse * inverse * inverse * (inner / units)
            for g in range(4):
                weighted = gains[g, pl.ds(0, 1), cols] * full[g, at, cols]
                raw[at, pl.ds(g * GW + first, width)] = (inverse * weighted - latent[g, at, cols] * scale).astype(bf16)

    loop(SLICE // 16, norm_back)
    for g in range(4):
        cols = pl.ds(g * GW, GW)
        slope[own_rows, cols] = dot(raw[:, cols], by_block[...]).astype(bf16)

    sides = (pl.ds(0, 2 * GW), pl.ds(2 * GW, 2 * GW))

    def block_rows(k, core):
        return pl.ds(pl.multiple_of(core * 320 + ((x + k + NX) % NX) * SLICE, 16), SLICE)

    for part in range(2):
        for side in range(2):
            cols = sides[part if side == 0 else 1 - part]
            view = slope.at[own_rows, cols]
            send(("a", 1, side, part), view, view, x_next[side])
    view = slope.at[own_rows, :]
    send(("ac", 0), view, view, other_core)
    scatter_next("q", 1)
    for side, back in ((0, -1), (1, 1)):
        view = slope.at[block_rows(back, c), sides[side]]
        recv(("a", 1, side, 0), view)
        send(("a", 2, side), view, view, x_next[side])
    gather_next("d", 0, 2)
    scatter_next("k", 2)
    for side, back in ((0, -1), (1, 1)):
        recv(("a", 1, side, 1), slope.at[block_rows(back, c), sides[1 - side]])
        view = slope.at[block_rows(back, c), :]
        send(("ac", 1 + side), view, view, other_core)
    for side in range(2):
        recv(("a", 2, side), slope.at[block_rows(2, c), sides[side]])
    view = slope.at[block_rows(2, c), :]
    send(("ac", 3), view, view, other_core)
    scatter_next("q", 2)
    for i, k in enumerate((0, -1, 1, 2)):
        recv(("ac", i), slope.at[block_rows(k, 1 - c), :])

    l_tok.wait()
    for g, partners in ((0, (4,)), (3, (3, 5)), (2, (2,)), (1, ())):
        out = dot(tok[...], slope[:, pl.ds(g * GW, GW)]).astype(bf16)
        for j in range(4):
            pd[g, j] = out[:, j * DB : (j + 1) * DB]
        for d in partners:
            scatter_pair("d", d)
    gather_next("d", 0, 3)

    def finish(refs, grad, mean, rows, cols):
        def step(i, squares):
            at = pl.ds(pl.multiple_of(i * 16, 16), 16)
            g = total(refs, at) / TOKENS
            mean[at, :] = beta_first * mean[at, :] + (1.0 - beta_first) * g
            return squares + g[0:8] * g[0:8] + g[8:16] * g[8:16]

        return lax.fori_loop(0, rows // 16, step, jnp.zeros((8, cols), f32))

    def heads_of(width, per_head):
        col = lax.broadcasted_iota(jnp.int32, (width, 128), 0)
        head = lax.broadcasted_iota(jnp.int32, (width, 128), 1)
        return ((col >= head * per_head) & (col < (head + 1) * per_head)).astype(f32).astype(bf16)

    def columns_of(width, per_head):
        head = lax.broadcasted_iota(jnp.int32, (128, width), 0)
        col = lax.broadcasted_iota(jnp.int32, (128, width), 1)
        return ((col >= head * per_head) & (col < (head + 1) * per_head)).astype(f32).astype(bf16)

    l_ek.wait()
    squares_k = finish(scatter_last("k"), None, ek, KR, KC)
    heads_k = jnp.sum(select_dot(squares_k, heads_of(KC, KVH)), axis=0, keepdims=True) / (KVL * KVH)
    scatter_first("d")
    gather_first("d", 1)
    l_eq.wait()
    squares_q = finish(scatter_last("q"), None, eq, QR, QC)
    heads_q = jnp.sum(select_dot(squares_q, heads_of(QC, QK)), axis=0, keepdims=True) / (QL * QK)
    row8 = lax.broadcasted_iota(jnp.int32, (8, 128), 0)
    small[...] = jnp.where(row8 == 0, heads_q, jnp.where(row8 == 1, heads_k, 0.0))
    send(("hy",), small, small_pair, other_half)
    for d in (6, 1, 7, 0):
        scatter_pair("d", d)
    scatter_next("d", 0)
    gather_next("d", 1, 1)
    recv(("hy",), small_pair)
    small_z[0] = small[...] + small_pair[...]
    for k in range(1, NZ):
        send(("hz", k), small_z.at[0], small_z.at[k], z_dev(k))
    gather_next("d", 0, 4)
    scatter_next("d", 1)
    gather_next("d", 1, 2)

    def token_grad():
        out = jnp.zeros((DC, TOK), f32)
        for g in range(4):
            rows = jnp.concatenate([wd[g, j] for j in range(4)], axis=1)
            out += dot_t(rows, slope[:, pl.ds(g * GW, GW)])
        tg[...] = out.astype(bf16)

    for k in range(1, NZ):
        recv(("hz", k), small_z.at[k])
    heads = small_z[0]
    for k in range(1, NZ):
        heads = heads + small_z[k]
    small_row[...] = jnp.zeros((8, 128), f32)
    small_row[pl.ds(0, 1), pl.ds(0, 8)] = sq_ref[...]
    small_row[pl.ds(1, 1), pl.ds(0, 8)] = sk_ref[...]
    second = beta_second * small_row[...] + (1.0 - beta_second) * heads
    osq_ref[...] = second[0:1, 0:8]
    osk_ref[...] = second[1:2, 0:8]

    def update(second_wide, mean, out, rows):
        factor = 1.0 / (jnp.sqrt(second_wide / second_scale) + adam_eps)

        def body(i):
            at = pl.ds(pl.multiple_of(i * 16, 16), 16)
            out[at, :] = mean[at, :] / first_scale * factor

        loop(rows // 16, body)

    update(select_dot(second, columns_of(QC, QK))[0:1], eq, mq, QR)
    update(select_dot(second, columns_of(KC, KVH))[1:2], ek, mk, KR)
    stores = [fetch(eq, nq_h), fetch(ek, nk_h), fetch(mq, uq_h), fetch(mk, uk_h)]

    scatter_next("d", 2)
    gather_next("d", 1, 3)
    eye = lax.broadcasted_iota(jnp.int32, (128, 128), 0) == lax.broadcasted_iota(jnp.int32, (128, 128), 1)
    small_row[...] = jnp.zeros((8, 128), f32)
    small_row[pl.ds(0, 1), pl.ds(0, QR)] = sdq_ref[...]
    small_row[pl.ds(0, 1), pl.ds(QR, KR)] = sdk_ref[...]
    old = small_row[pl.ds(0, 1), :]
    for load in l_ed:
        load.wait()
    grad = total(scatter_last("d"), slice(None)).T / TOKENS
    mean_next = beta_first * ed[...] + (1.0 - beta_first) * grad
    ed[...] = mean_next
    column = jnp.sum(grad * grad, axis=1, keepdims=True) / D
    row = jnp.sum(jnp.where(eye, column, 0.0), axis=0, keepdims=True)
    small_core[0] = jnp.broadcast_to(row, (8, 128))
    send(("rc",), small_core.at[0], small_core.at[1], other_core)
    stores += [fetch(ed.at[pl.ds(0, QR)], ndq_h), fetch(ed.at[pl.ds(QR, KR)], ndk_h)]
    gather_next("d", 1, 4)
    recv(("rc",), small_core.at[1])
    small_x[0] = small_core[0] + small_core[1]
    for k in range(1, 2 * NX):
        send(("rx", k), small_x.at[0], small_x.at[k], head_dev(k))
    token_grad()
    stores += [fetch(tg, tg_h)]
    for k in range(1, 2 * NX):
        recv(("rx", k), small_x.at[k])
    rows_total = small_x[0]
    for k in range(1, 2 * NX):
        rows_total = rows_total + small_x[k]
    second_row = beta_second * old + (1.0 - beta_second) * rows_total[0:1]
    osdq_ref[...] = second_row[:, 0:QR]
    osdk_ref[...] = second_row[:, QR:DB]
    second_col = jnp.sum(jnp.where(eye, second_row, 0.0), axis=1, keepdims=True)
    factor = 1.0 / (jnp.sqrt(second_col / second_scale) + adam_eps)
    md[...] = mean_next / first_scale * factor
    stores += [fetch(md.at[pl.ds(0, QR)], udq_h), fetch(md.at[pl.ds(QR, KR)], udk_h)]

    for copy in sent:
        copy.wait_send()
    for store in stores:
        store.wait()


def publish(*refs):
    n = (len(refs) - 2) // 3
    into = [pltpu.make_async_copy(refs[i], refs[2 * n + i], refs[-2].at[i]) for i in range(n)]
    out = [pltpu.make_async_copy(refs[2 * n + i], refs[n + i], refs[-1].at[i]) for i in range(n)]
    for copy in into:
        copy.start()
    for i in range(n):
        into[i].wait()
        out[i].start()
    for copy in out:
        copy.wait()


def local(*args):
    (
        tokens, query_latent, keyval_latent, query_gain, keyval_gain, query_cotangent, keyval_cotangent,
        master_query_up, master_keyval_up, master_query_down, master_keyval_down,
        mean_query_up, mean_keyval_up, mean_query_down, mean_keyval_down,
        square_query_up, square_keyval_up, square_query_down, square_keyval_down,
    ) = args
    hbm = pl.BlockSpec(memory_space=pl.ANY)
    vmem = pl.BlockSpec(memory_space=pltpu.VMEM)

    def shape(rows, cols, kind=f32):
        return jax.ShapeDtypeStruct((rows, cols), kind)

    V = pltpu.VMEM
    outs = pl.pallas_call(
        kernel,
        name="backward_and_update",
        out_shape=(
            shape(DC, TOK, bf16),
            shape(QR, QC), shape(KR, KC), shape(QR, DC), shape(KR, DC),
            shape(QR, QC), shape(KR, KC), shape(QR, DC), shape(KR, DC),
            shape(1, 8), shape(1, 8), shape(1, QR), shape(1, KR),
        ),
        in_specs=[hbm] * 3 + [vmem] * 2 + [hbm] * 10 + [vmem] * 4,
        out_specs=(hbm,) * 9 + (vmem,) * 4,
        scratch_shapes=[
            V((DC, TOK), bf16), V((TOK, QL), bf16), V((TOK, KVL), bf16), V((TOK, QC), bf16), V((TOK, KC), bf16),
            V((QR, QC), f32), V((KR, KC), f32), V((DB, DC), f32),
            V((QR, QC), f32), V((KR, KC), f32), V((DB, DC), f32),
            V((4, 4, QR, QC), bf16), V((4, 4, KR, KC), bf16), V((4, 4, DC, DB), bf16),
            V((16, QR, QC), bf16), V((16, KR, KC), bf16), V((4, 4, DC, DB), bf16),
            V((8, QR, QC), bf16), V((8, KR, KC), bf16), V((8, DC, DB), bf16),
            V((2, 4, QR, QC), bf16), V((2, 4, KR, KC), bf16), V((2, 4, DC, DB), bf16),
            V((TOK, QL), bf16), V((TOK, KVL), bf16), V((GW, TOK), bf16),
            V((4, TOK, GW), bf16), V((4, 320, GW), bf16), V((4, 320, GW), bf16),
            V((4, 3, SLICE, GW), bf16), V((4, SLICE, GW), bf16), V((4, SLICE, GW), bf16), V((4, SLICE, GW), f32),
            V((4, SLICE, GW), f32), V((4, 8, GW), f32), V((GW, GW), bf16), V((SLICE, 4 * GW), bf16),
            V((TOK, 4 * GW), bf16), V((DC, TOK), bf16),
            V((8, 128), f32), V((8, 128), f32), V((8, 8, 128), f32), V((8, 128), f32),
            V((2, 8, 128), f32), V((8, 8, 128), f32),
            V((1, QL), f32), V((1, KVL), f32),
            pltpu.SemaphoreType.DMA((N_SEM,)), pltpu.SemaphoreType.DMA((N_SEM,)), pltpu.SemaphoreType.DMA((32,)),
        ],
        compiler_params=pltpu.CompilerParams(
            collective_id=0, has_side_effects=True, vmem_limit_bytes=62 * 2**20
        ),
        cost_estimate=pl.CostEstimate(flops=11 * 10**9, bytes_accessed=14 * 10**6, transcendentals=0),
    )(
        tokens.T, query_latent, keyval_latent, query_gain, keyval_gain,
        query_cotangent, keyval_cotangent,
        master_query_up, master_keyval_up, master_query_down, master_keyval_down,
        mean_query_up, mean_keyval_up, mean_query_down, mean_keyval_down,
        square_query_up.reshape(1, 8), square_keyval_up.reshape(1, 8),
        square_query_down.reshape(1, QR), square_keyval_down.reshape(1, KR),
    )
    outs = pl.pallas_call(
        publish,
        name="publish",
        out_shape=tuple(jax.ShapeDtypeStruct(o.shape, o.dtype) for o in outs),
        in_specs=[hbm] * len(outs),
        out_specs=(hbm,) * len(outs),
        scratch_shapes=[V(o.shape, o.dtype) for o in outs]
        + [pltpu.SemaphoreType.DMA((len(outs),)), pltpu.SemaphoreType.DMA((len(outs),))],
    )(*outs)
    return (
        outs[0].T, *outs[1:9],
        outs[9].reshape(8), outs[10].reshape(8), outs[11].reshape(QR), outs[12].reshape(KR),
    )


def solution(mesh):
    both = P("dp", "head")
    return jax.shard_map(
        local,
        mesh=mesh,
        in_specs=(both, P("dp", None), P("dp", None), P(), P()) + (both,) * 10
        + (P("head"), P("head"), P("dp"), P("dp")),
        out_specs=(both,) * 9 + (P("head"), P("head"), P("dp"), P("dp")),
        check_vma=False,
    )
```

```python
import jax
import jax.numpy as jnp
from jax import lax
from jax.experimental import pallas as pl
from jax.experimental.pallas import tpu as pltpu
from jax.sharding import PartitionSpec as P

D = 7168
QL = 1536
KVL = 512
QK = 192
KVH = 256
TOKENS = 10240
TOK = 640

NZ = 8
NX = 4
DC = 448
QR, KR, DR = 96, 32, 448
GQ, GK, GW = 4 * QR, 4 * KR, 4 * (QR + KR)
QC, KC = 1536, 2048
DB = QR + KR
FAR = 256
SLICE = 80

norm_eps = 1e-06
adam_eps = 1e-08
beta_first = 0.9
beta_second = 0.95
adam_step = 10
first_scale = 1.0 - beta_first**adam_step
second_scale = 1.0 - beta_second**adam_step

MESH = pl.DeviceIdType.MESH
f32 = jnp.float32
bf16 = jnp.bfloat16
N_SEM = 192


def place(rel, d):
    d = d % NZ
    if d == 0 or d == NZ // 2:
        return (0, rel * 2 + (1 if d else 0))
    if d < NZ // 2:
        return (d, rel * 2)
    return (NZ - d, rel * 2 + 1)


def split3(a):
    hi = a.astype(bf16)
    rest = a - hi.astype(f32)
    mid = rest.astype(bf16)
    low = (rest - mid.astype(f32)).astype(bf16)
    return hi, mid, low


def dot(a, b):
    return jnp.dot(a, b, preferred_element_type=f32)


def dot_t(a, b):
    return lax.dot_general(a, b, (((1,), (1,)), ((), ())), preferred_element_type=f32)


def select_dot(a, chosen):
    hi, mid, low = split3(a)
    return dot(hi, chosen) + dot(mid, chosen) + dot(low, chosen)


def loop(count, body):
    def step(i, carry):
        body(i)
        return carry

    lax.fori_loop(0, count, step, 0)


def total(refs, rows):
    parts = [r[rows, :].astype(f32) for r in refs]
    out = parts[0]
    for p in parts[1:]:
        out = out + p
    return out


def add_into(refs, out, start, rows):
    def body(i):
        at = pl.ds(pl.multiple_of(start + i * 16, 16), 16)
        out[at, :] = total(refs, at).astype(out.dtype)

    loop(rows // 16, body)


def kernel(
    tok_h, lq_h, lk_h, gq_ref, gk_ref, cq_h, ck_h,
    mq_h, mk_h, mdq_h, mdk_h, eq_h, ek_h, edq_h, edk_h,
    sq_ref, sk_ref, sdq_ref, sdk_ref,
    tg_h, uq_h, uk_h, udq_h, udk_h, nq_h, nk_h, ndq_h, ndk_h,
    osq_ref, osk_ref, osdq_ref, osdk_ref,
    tok, lq, lk, cq, ck, mq, mk, md, eq, ek, ed,
    wq, wk, wd, pq, pk, pd, yq, yk, yd, zq, zk, zd,
    normq, normk, turned, up, core_in, half, x_in, mine, pair_in, full,
    latent, gains, by_block, raw, slope, tg, small, small_pair, small_z, small_row, small_core, small_x,
    gq_row, gk_row, send_sems, recv_sems, local_sems,
):
    dp = lax.axis_index("dp")
    hd = lax.axis_index("head")
    yh, z = dp // NZ, dp % NZ
    x, yl, c = hd // 4, (hd // 2) % 2, hd % 2

    def z_dev(k):
        return (yh * NZ + (z + k + NZ) % NZ, hd)

    def x_dev(k):
        return (dp, ((x + k + NX) % NX) * 4 + yl * 2 + c)

    def head_dev(k):
        low = 1 - yl if k >= NX else yl
        return (dp, ((x + k) % NX) * 4 + low * 2 + c)

    other_half = ((1 - yh) * NZ + z, hd)
    other_low = (dp, x * 4 + (1 - yl) * 2 + c)
    other_core = (dp, x * 4 + yl * 2 + 1 - c)
    z_next = (z_dev(1), z_dev(-1))
    x_next = (x_dev(1), x_dev(-1))

    ids = {}
    sent = []

    def remote(key, src, dst, dev):
        i = ids.setdefault(key, len(ids))
        return pltpu.make_async_remote_copy(
            src_ref=src, dst_ref=dst, send_sem=send_sems.at[i], recv_sem=recv_sems.at[i],
            device_id=dev, device_id_type=MESH,
        )

    def send(key, src, dst, dev):
        copy = remote(key, src, dst, dev)
        copy.start()
        sent.append(copy)

    def recv(key, land):
        remote(key, land, land, other_core).wait_recv()

    n_local = [0]

    def fetch(src, dst):
        copy = pltpu.make_async_copy(src, dst, local_sems.at[n_local[0]])
        n_local[0] += 1
        copy.start()
        return copy

    gq_row[...] = gq_ref[...].reshape(1, QL)
    gk_row[...] = gk_ref[...].reshape(1, KVL)
    l_mk, l_mq = fetch(mk_h, mk), fetch(mq_h, mq)
    l_lk, l_ck = fetch(lk_h, lk), fetch(ck_h, ck)
    l_lq, l_cq = fetch(lq_h, lq), fetch(cq_h, cq)
    l_md = (fetch(mdq_h, md.at[pl.ds(0, QR)]), fetch(mdk_h, md.at[pl.ds(QR, KR)]))
    l_tok = fetch(tok_h, tok)
    l_eq, l_ek = fetch(eq_h, eq), fetch(ek_h, ek)
    l_ed = (fetch(edq_h, ed.at[pl.ds(0, QR)]), fetch(edk_h, ed.at[pl.ds(QR, KR)]))

    barrier = pltpu.get_barrier_semaphore()
    peers = [z_dev(k) for k in range(1, NZ)] + [head_dev(k) for k in range(1, 2 * NX)]
    peers += [other_half, other_core]
    for dev in peers:
        pl.semaphore_signal(barrier, inc=1, device_id=dev, device_id_type=MESH)

    def round_rows(src, dst, rows):
        def body(i):
            at = pl.ds(pl.multiple_of(i * 16, 16), 16)
            dst[at, :] = src[at, :].astype(bf16)

        loop(rows // 16, body)

    gathered = {"k": (wk, KR), "q": (wq, QR), "d": (wd, DR)}

    def gather_pair(w):
        ref, _ = gathered[w]
        send(("y", w), ref.at[place(0, 0)], ref.at[place(1, 0)], other_half)

    def round_z(w, rel, ref):
        return ref.at[:, pl.ds(0, QC - FAR)] if w == "q" and rel else ref

    def gather_first(w, rel):
        ref, _ = gathered[w]
        if rel:
            recv(("y", w), ref.at[place(1, 0)])
        for side, sign in ((0, -1), (1, 1)):
            here, there = ref.at[place(rel, 0)], ref.at[place(rel, sign)]
            send(("g", w, rel, 1, side), round_z(w, rel, here), round_z(w, rel, there), z_next[side])

    def cross(d):
        far = pl.ds(QC - FAR, FAR)
        send(("b", d), wq.at[place(0, d)].at[:, far], wq.at[place(1, d)].at[:, far], other_half)

    def crossed(d):
        recv(("b", d), wq.at[place(1, d)].at[:, pl.ds(QC - FAR, FAR)])

    def gather_next(w, rel, step):
        ref, rows = gathered[w]
        h = rows // 2
        for side, sign in ((0, -1), (1, 1)):
            here = round_z(w, rel, ref.at[place(rel, sign * step)])
            if step == 4:
                recv(("g", w, rel, 4, side), here.at[pl.ds(side * h, h)])
                continue
            recv(("g", w, rel, step, side), here)
            there = round_z(w, rel, ref.at[place(rel, sign * (step + 1))])
            if step == 3:
                here, there = here.at[pl.ds(side * h, h)], there.at[pl.ds(side * h, h)]
            send(("g", w, rel, step + 1, side), here, there, z_next[side])
        if w == "q" and rel == 0 and step < 4:
            cross(step)
            cross(NZ - step)

    def far_half(d, side):
        return wq.at[place(1, d)].at[pl.ds(side * (QR // 2), QR // 2), pl.ds(QC - FAR, FAR)]

    def own_block(ref, half_of, d):
        return ref.at[half_of * NZ + (z + d) % NZ]

    scattered = {
        "k": (lambda d: own_block(pk, yh, d), lambda d: own_block(pk, 1 - yh, d), yk, zk, KR),
        "q": (lambda d: own_block(pq, yh, d), lambda d: own_block(pq, 1 - yh, d), yq, zq, QR),
        "d": (lambda d: pd.at[place(0, d)], lambda d: pd.at[place(1, d)], yd, zd, DR),
    }

    def scatter_pair(w, d):
        _, theirs, y, _, _ = scattered[w]
        send(("sy", w, d), theirs(d), y.at[d], other_half)

    def scatter_first(w):
        own, _, y, zz, rows = scattered[w]
        h = rows // 2
        recv(("sy", w, 4), y.at[4])
        add_into([own(4), y.at[4]], own(4), 0, rows)
        for side in range(2):
            at = pl.ds(side * h, h)
            send(("s", w, 0, side), own(4).at[at], zz.at[side, 0].at[at], z_next[side])

    def scatter_next(w, step):
        own, _, y, zz, rows = scattered[w]
        h = rows // 2
        for side in range(2):
            d = 3 - step if side == 0 else 5 + step
            recv(("sy", w, d), y.at[d])
            if step == 0:
                came = zz.at[side, 0]
                recv(("s", w, 0, side), came.at[pl.ds(side * h, h)])
                add_into([own(d), y.at[d], came], own(d), side * h, h)
                add_into([own(d), y.at[d]], own(d), (1 - side) * h, h)
            else:
                came = zz.at[side, step]
                recv(("s", w, step, side), came)
                add_into([own(d), y.at[d], came], own(d), 0, rows)
            send(("s", w, step + 1, side), own(d), zz.at[side, step + 1], z_next[side])

    def scatter_last(w):
        own, _, y, zz, _ = scattered[w]
        recv(("sy", w, 0), y.at[0])
        recv(("s", w, 3, 0), zz.at[0, 3])
        recv(("s", w, 3, 1), zz.at[1, 3])
        return [own(0), y.at[0], zz.at[0, 3], zz.at[1, 3]]

    l_mk.wait()
    round_rows(mk, wk.at[place(0, 0)], KR)
    l_mq.wait()
    round_rows(mq, wq.at[place(0, 0)], QR)
    pl.semaphore_wait(barrier, len(peers))
    gather_pair("k")
    gather_first("k", 0)
    gather_pair("q")
    gather_first("q", 0)
    for load in l_md:
        load.wait()
    wd[place(0, 0)] = md[...].T.astype(bf16)

    def normalize(src, gain_ref, dst, width):
        def body(i):
            at = pl.ds(pl.multiple_of(i * 32, 32), 32)
            values = src[at, :].astype(f32)
            inverse = lax.rsqrt(jnp.sum(values * values, axis=1, keepdims=True) / width + norm_eps)
            dst[at, :] = (values * inverse * gain_ref[...]).astype(bf16)

        loop(TOK // 32, body)

    def turn(src, start, width):
        def body(i):
            at = pl.ds(pl.multiple_of(i * 128, 128), 128)
            block = src[at, pl.ds(start, width)]
            turned[pl.ds(0, width), at] = block.T

        loop(TOK // 128, body)

    def part_keyval(half_of):
        turn(normk, pl.multiple_of(half_of * 256, 128), 256)

        def body(i):
            at = pl.ds(pl.multiple_of(i * 512, 512), 512)
            out = dot(turned[pl.ds(0, 256), :], ck[:, at]).astype(bf16)
            pk[pl.ds(half_of * NZ, NZ), :, at] = out.reshape(NZ, KR, 512)

        loop(KC // 512, body)

    def part_query(half_of):
        def chunk(q):
            turn(normq, pl.multiple_of(half_of * 768 + q * GQ, 128), GQ)

            def body(i):
                at = pl.ds(pl.multiple_of(i * 512, 512), 512)
                out = dot(turned[pl.ds(0, GQ), :], cq[:, at]).astype(bf16)
                pq[pl.ds(half_of * NZ + q * 4, 4), :, at] = out.reshape(4, QR, 512)

            loop(QC // 512, body)

        loop(2, chunk)

    first_token = pl.multiple_of(c * (TOK // 2) + x * SLICE, 16)

    def arrange(src, gain_ref, rows, natural, width, group, at):
        lane = lax.broadcasted_iota(jnp.int32, (1, 4 * rows), 1)
        j = sum((lane >= rows * k).astype(jnp.int32) for k in (1, 2, 3))
        inside = lane - j * rows
        rel, back = j // 2, j % 2
        d = back * (NZ // 2) if group == 0 else jnp.where(back == 1, NZ - group, group)
        owner = jnp.where(rel == 1, 1 - yh, yh) * NZ + (z + d) % NZ
        source = owner * rows + inside
        chosen = (lax.broadcasted_iota(jnp.int32, (width, 4 * rows), 0) == source).astype(f32).astype(bf16)
        latent[group, :, at] = dot(src[pl.ds(first_token, SLICE), :], chosen)
        gain = jnp.broadcast_to(gain_ref[...], (8, width))
        gains[group, :, at] = select_dot(gain, chosen)

    def arrange_blocks():
        col = lax.broadcasted_iota(jnp.int32, (1, GW), 1)
        j = sum((col >= DB * k).astype(jnp.int32) for k in (1, 2, 3))
        inside = col - j * DB
        source = jnp.where(inside < QR, j * QR + inside, GQ + j * KR + inside - QR)
        by_block[...] = (lax.broadcasted_iota(jnp.int32, (GW, GW), 0) == source).astype(f32).astype(bf16)

    def arrange_group(g):
        arrange(lq, gq_row, QR, 0, QL, g, pl.ds(0, GQ))
        arrange(lk, gk_row, KR, 0, KVL, g, pl.ds(GQ, GK))

    def upstream(g):
        if g:
            crossed(g)
            crossed(NZ - g)
        for side, d in ((0, -3), (1, 3)):
            if g == 3:
                send(("bf", side), far_half(d, side), far_half(4, side), z_next[side])
            if g == 0:
                recv(("bf", side), far_half(4, side))

        def body(i):
            at = pl.ds(pl.multiple_of(i * 640, 640), 640)
            up[g, at, pl.ds(0, GQ)] = dot_t(cq[at, :], wq[g].reshape(GQ, QC)).astype(bf16)
            up[g, at, pl.ds(GQ, GK)] = dot_t(ck[at, :], wk[g].reshape(GK, KC)).astype(bf16)

        loop(TOK // 640, body)
        there = pl.ds(pl.multiple_of((1 - c) * 320, 16), 320)
        send(("c", g), up.at[g, there], core_in.at[g], other_core)

    def after_core(g):
        recv(("c", g), core_in.at[g])
        here = up.at[g, pl.ds(pl.multiple_of(c * 320, 16), 320)]
        add_into([here, core_in.at[g]], half.at[g], 0, 320)
        for k in (2, 1, 3):
            to = (x + k) % NX
            send(("x", g, k), half.at[g, pl.ds(pl.multiple_of(to * SLICE, 16), SLICE)], x_in.at[g, k - 1], x_dev(k))

    def after_x(g):
        for k in range(1, NX):
            recv(("x", g, k), x_in.at[g, k - 1])
        here = half.at[g, pl.ds(pl.multiple_of(x * SLICE, 16), SLICE)]
        add_into([here] + [x_in.at[g, k] for k in range(NX - 1)], mine.at[g], 0, SLICE)
        send(("l", g), mine.at[g], pair_in.at[g], other_low)

    def after_low(g):
        recv(("l", g), pair_in.at[g])
        add_into([mine.at[g], pair_in.at[g]], full.at[g], 0, SLICE)

    l_lk.wait()
    normalize(lk, gk_row, normk, KVL)
    l_ck.wait()
    part_keyval(1 - yh)
    for d in (4, 3, 5):
        scatter_pair("k", d)
    gather_first("k", 1)
    l_lq.wait()
    normalize(lq, gq_row, normq, QL)
    gather_first("q", 1)
    gather_next("k", 0, 1)
    gather_next("q", 0, 1)
    l_cq.wait()
    part_query(1 - yh)
    scatter_pair("q", 4)
    gather_next("k", 1, 1)
    gather_next("q", 1, 1)
    scatter_pair("q", 3)
    upstream(1)

    gather_next("k", 0, 2)
    after_core(1)
    part_keyval(yh)
    gather_next("q", 0, 2)
    scatter_pair("q", 5)
    gather_next("k", 1, 2)
    scatter_pair("k", 2)
    gather_next("q", 1, 2)
    after_x(1)
    scatter_pair("q", 2)
    upstream(2)

    gather_next("k", 0, 3)
    after_core(2)
    part_query(yh)
    gather_next("q", 0, 3)
    scatter_pair("k", 6)
    gather_next("k", 1, 3)
    scatter_pair("q", 6)
    arrange_blocks()
    arrange_group(0)
    arrange_group(1)
    gather_next("q", 1, 3)
    after_x(2)
    scatter_pair("q", 1)
    upstream(3)

    gather_next("k", 0, 4)
    after_core(3)
    gather_next("q", 0, 4)
    scatter_first("k")
    gather_next("k", 1, 4)
    scatter_first("q")
    after_low(1)
    gather_next("q", 1, 4)
    gather_first("d", 0)
    upstream(0)
    after_x(3)
    scatter_next("k", 0)
    after_core(0)
    scatter_next("q", 0)
    gather_next("d", 0, 1)
    after_x(0)
    scatter_pair("k", 1)
    scatter_pair("k", 7)
    scatter_pair("q", 7)
    scatter_pair("k", 0)
    gather_pair("d")
    scatter_pair("q", 0)
    arrange_group(2)
    arrange_group(3)
    scatter_next("k", 1)
    for g in (2, 3, 0):
        after_low(g)

    own_rows = pl.ds(first_token, SLICE)

    def norm_back(i):
        at = pl.ds(pl.multiple_of(i * 16, 16), 16)
        for first, width, units in ((0, GQ, QL), (GQ, GK, KVL)):
            cols = pl.ds(first, width)
            squares = 0.0
            inner = 0.0
            for g in range(4):
                values = latent[g, at, cols]
                squares += jnp.sum(values * values, axis=1, keepdims=True)
                inner += jnp.sum(values * gains[g, pl.ds(0, 1), cols] * full[g, at, cols], axis=1, keepdims=True)
            inverse = lax.rsqrt(squares / units + norm_eps)
            scale = inverse * inverse * inverse * (inner / units)
            for g in range(4):
                weighted = gains[g, pl.ds(0, 1), cols] * full[g, at, cols]
                raw[at, pl.ds(g * GW + first, width)] = (inverse * weighted - latent[g, at, cols] * scale).astype(bf16)

    loop(SLICE // 16, norm_back)
    for g in range(4):
        cols = pl.ds(g * GW, GW)
        slope[own_rows, cols] = dot(raw[:, cols], by_block[...]).astype(bf16)

    sides = (pl.ds(0, 2 * GW), pl.ds(2 * GW, 2 * GW))

    def block_rows(k, core):
        return pl.ds(pl.multiple_of(core * 320 + ((x + k + NX) % NX) * SLICE, 16), SLICE)

    for part in range(2):
        for side in range(2):
            cols = sides[part if side == 0 else 1 - part]
            view = slope.at[own_rows, cols]
            send(("a", 1, side, part), view, view, x_next[side])
    view = slope.at[own_rows, :]
    send(("ac", 0), view, view, other_core)
    scatter_next("q", 1)
    for side, back in ((0, -1), (1, 1)):
        view = slope.at[block_rows(back, c), sides[side]]
        recv(("a", 1, side, 0), view)
        send(("a", 2, side), view, view, x_next[side])
    gather_next("d", 0, 2)
    scatter_next("k", 2)
    for side, back in ((0, -1), (1, 1)):
        recv(("a", 1, side, 1), slope.at[block_rows(back, c), sides[1 - side]])
        view = slope.at[block_rows(back, c), :]
        send(("ac", 1 + side), view, view, other_core)
    for side in range(2):
        recv(("a", 2, side), slope.at[block_rows(2, c), sides[side]])
    view = slope.at[block_rows(2, c), :]
    send(("ac", 3), view, view, other_core)
    scatter_next("q", 2)
    for i, k in enumerate((0, -1, 1, 2)):
        recv(("ac", i), slope.at[block_rows(k, 1 - c), :])

    l_tok.wait()
    for g, partners in ((0, (4,)), (3, (3, 5)), (2, (2,)), (1, ())):
        out = dot(tok[...], slope[:, pl.ds(g * GW, GW)]).astype(bf16)
        for j in range(4):
            pd[g, j] = out[:, j * DB : (j + 1) * DB]
        for d in partners:
            scatter_pair("d", d)
    gather_next("d", 0, 3)

    def finish(refs, grad, mean, rows, cols):
        def step(i, squares):
            at = pl.ds(pl.multiple_of(i * 16, 16), 16)
            g = total(refs, at) / TOKENS
            mean[at, :] = beta_first * mean[at, :] + (1.0 - beta_first) * g
            return squares + g[0:8] * g[0:8] + g[8:16] * g[8:16]

        return lax.fori_loop(0, rows // 16, step, jnp.zeros((8, cols), f32))

    def heads_of(width, per_head):
        col = lax.broadcasted_iota(jnp.int32, (width, 128), 0)
        head = lax.broadcasted_iota(jnp.int32, (width, 128), 1)
        return ((col >= head * per_head) & (col < (head + 1) * per_head)).astype(f32).astype(bf16)

    def columns_of(width, per_head):
        head = lax.broadcasted_iota(jnp.int32, (128, width), 0)
        col = lax.broadcasted_iota(jnp.int32, (128, width), 1)
        return ((col >= head * per_head) & (col < (head + 1) * per_head)).astype(f32).astype(bf16)

    l_ek.wait()
    squares_k = finish(scatter_last("k"), None, ek, KR, KC)
    heads_k = jnp.sum(select_dot(squares_k, heads_of(KC, KVH)), axis=0, keepdims=True) / (KVL * KVH)
    scatter_first("d")
    gather_first("d", 1)
    l_eq.wait()
    squares_q = finish(scatter_last("q"), None, eq, QR, QC)
    heads_q = jnp.sum(select_dot(squares_q, heads_of(QC, QK)), axis=0, keepdims=True) / (QL * QK)
    row8 = lax.broadcasted_iota(jnp.int32, (8, 128), 0)
    small[...] = jnp.where(row8 == 0, heads_q, jnp.where(row8 == 1, heads_k, 0.0))
    send(("hy",), small, small_pair, other_half)
    for d in (6, 1, 7, 0):
        scatter_pair("d", d)
    scatter_next("d", 0)
    gather_next("d", 1, 1)
    recv(("hy",), small_pair)
    small_z[0] = small[...] + small_pair[...]
    for k in range(1, NZ):
        send(("hz", k), small_z.at[0], small_z.at[k], z_dev(k))
    gather_next("d", 0, 4)
    scatter_next("d", 1)
    gather_next("d", 1, 2)

    def token_grad():
        out = jnp.zeros((DC, TOK), f32)
        for g in range(4):
            rows = jnp.concatenate([wd[g, j] for j in range(4)], axis=1)
            out += dot_t(rows, slope[:, pl.ds(g * GW, GW)])
        tg[...] = out.astype(bf16)

    for k in range(1, NZ):
        recv(("hz", k), small_z.at[k])
    heads = small_z[0]
    for k in range(1, NZ):
        heads = heads + small_z[k]
    small_row[...] = jnp.zeros((8, 128), f32)
    small_row[pl.ds(0, 1), pl.ds(0, 8)] = sq_ref[...]
    small_row[pl.ds(1, 1), pl.ds(0, 8)] = sk_ref[...]
    second = beta_second * small_row[...] + (1.0 - beta_second) * heads
    osq_ref[...] = second[0:1, 0:8]
    osk_ref[...] = second[1:2, 0:8]

    def update(second_wide, mean, out, rows):
        factor = 1.0 / (jnp.sqrt(second_wide / second_scale) + adam_eps)

        def body(i):
            at = pl.ds(pl.multiple_of(i * 16, 16), 16)
            out[at, :] = mean[at, :] / first_scale * factor

        loop(rows // 16, body)

    update(select_dot(second, columns_of(QC, QK))[0:1], eq, mq, QR)
    update(select_dot(second, columns_of(KC, KVH))[1:2], ek, mk, KR)
    stores = [fetch(eq, nq_h), fetch(ek, nk_h), fetch(mq, uq_h), fetch(mk, uk_h)]

    scatter_next("d", 2)
    gather_next("d", 1, 3)
    eye = lax.broadcasted_iota(jnp.int32, (128, 128), 0) == lax.broadcasted_iota(jnp.int32, (128, 128), 1)
    small_row[...] = jnp.zeros((8, 128), f32)
    small_row[pl.ds(0, 1), pl.ds(0, QR)] = sdq_ref[...]
    small_row[pl.ds(0, 1), pl.ds(QR, KR)] = sdk_ref[...]
    old = small_row[pl.ds(0, 1), :]
    for load in l_ed:
        load.wait()
    grad = total(scatter_last("d"), slice(None)).T / TOKENS
    mean_next = beta_first * ed[...] + (1.0 - beta_first) * grad
    ed[...] = mean_next
    column = jnp.sum(grad * grad, axis=1, keepdims=True) / D
    row = jnp.sum(jnp.where(eye, column, 0.0), axis=0, keepdims=True)
    small_core[0] = jnp.broadcast_to(row, (8, 128))
    send(("rc",), small_core.at[0], small_core.at[1], other_core)
    stores += [fetch(ed.at[pl.ds(0, QR)], ndq_h), fetch(ed.at[pl.ds(QR, KR)], ndk_h)]
    gather_next("d", 1, 4)
    recv(("rc",), small_core.at[1])
    small_x[0] = small_core[0] + small_core[1]
    for k in range(1, 2 * NX):
        send(("rx", k), small_x.at[0], small_x.at[k], head_dev(k))
    token_grad()
    stores += [fetch(tg, tg_h)]
    for k in range(1, 2 * NX):
        recv(("rx", k), small_x.at[k])
    rows_total = small_x[0]
    for k in range(1, 2 * NX):
        rows_total = rows_total + small_x[k]
    second_row = beta_second * old + (1.0 - beta_second) * rows_total[0:1]
    osdq_ref[...] = second_row[:, 0:QR]
    osdk_ref[...] = second_row[:, QR:DB]
    second_col = jnp.sum(jnp.where(eye, second_row, 0.0), axis=1, keepdims=True)
    factor = 1.0 / (jnp.sqrt(second_col / second_scale) + adam_eps)
    md[...] = mean_next / first_scale * factor
    stores += [fetch(md.at[pl.ds(0, QR)], udq_h), fetch(md.at[pl.ds(QR, KR)], udk_h)]

    for copy in sent:
        copy.wait_send()
    for store in stores:
        store.wait()


def publish(*refs):
    n = (len(refs) - 2) // 3
    into = [pltpu.make_async_copy(refs[i], refs[2 * n + i], refs[-2].at[i]) for i in range(n)]
    out = [pltpu.make_async_copy(refs[2 * n + i], refs[n + i], refs[-1].at[i]) for i in range(n)]
    for copy in into:
        copy.start()
    for i in range(n):
        into[i].wait()
        out[i].start()
    for copy in out:
        copy.wait()


def local(*args):
    (
        tokens, query_latent, keyval_latent, query_gain, keyval_gain, query_cotangent, keyval_cotangent,
        master_query_up, master_keyval_up, master_query_down, master_keyval_down,
        mean_query_up, mean_keyval_up, mean_query_down, mean_keyval_down,
        square_query_up, square_keyval_up, square_query_down, square_keyval_down,
    ) = args
    hbm = pl.BlockSpec(memory_space=pl.ANY)
    vmem = pl.BlockSpec(memory_space=pltpu.VMEM)

    def shape(rows, cols, kind=f32):
        return jax.ShapeDtypeStruct((rows, cols), kind)

    V = pltpu.VMEM
    outs = pl.pallas_call(
        kernel,
        name="backward_and_update",
        out_shape=(
            shape(DC, TOK, bf16),
            shape(QR, QC), shape(KR, KC), shape(QR, DC), shape(KR, DC),
            shape(QR, QC), shape(KR, KC), shape(QR, DC), shape(KR, DC),
            shape(1, 8), shape(1, 8), shape(1, QR), shape(1, KR),
        ),
        in_specs=[hbm] * 3 + [vmem] * 2 + [hbm] * 10 + [vmem] * 4,
        out_specs=(hbm,) * 9 + (vmem,) * 4,
        scratch_shapes=[
            V((DC, TOK), bf16), V((TOK, QL), bf16), V((TOK, KVL), bf16), V((TOK, QC), bf16), V((TOK, KC), bf16),
            V((QR, QC), f32), V((KR, KC), f32), V((DB, DC), f32),
            V((QR, QC), f32), V((KR, KC), f32), V((DB, DC), f32),
            V((4, 4, QR, QC), bf16), V((4, 4, KR, KC), bf16), V((4, 4, DC, DB), bf16),
            V((16, QR, QC), bf16), V((16, KR, KC), bf16), V((4, 4, DC, DB), bf16),
            V((8, QR, QC), bf16), V((8, KR, KC), bf16), V((8, DC, DB), bf16),
            V((2, 4, QR, QC), bf16), V((2, 4, KR, KC), bf16), V((2, 4, DC, DB), bf16),
            V((TOK, QL), bf16), V((TOK, KVL), bf16), V((GW, TOK), bf16),
            V((4, TOK, GW), bf16), V((4, 320, GW), bf16), V((4, 320, GW), bf16),
            V((4, 3, SLICE, GW), bf16), V((4, SLICE, GW), bf16), V((4, SLICE, GW), bf16), V((4, SLICE, GW), f32),
            V((4, SLICE, GW), f32), V((4, 8, GW), f32), V((GW, GW), bf16), V((SLICE, 4 * GW), bf16),
            V((TOK, 4 * GW), bf16), V((DC, TOK), bf16),
            V((8, 128), f32), V((8, 128), f32), V((8, 8, 128), f32), V((8, 128), f32),
            V((2, 8, 128), f32), V((8, 8, 128), f32),
            V((1, QL), f32), V((1, KVL), f32),
            pltpu.SemaphoreType.DMA((N_SEM,)), pltpu.SemaphoreType.DMA((N_SEM,)), pltpu.SemaphoreType.DMA((32,)),
        ],
        compiler_params=pltpu.CompilerParams(
            collective_id=0, has_side_effects=True, vmem_limit_bytes=62 * 2**20
        ),
        cost_estimate=pl.CostEstimate(flops=11 * 10**9, bytes_accessed=14 * 10**6, transcendentals=0),
    )(
        tokens.T, query_latent, keyval_latent, query_gain, keyval_gain,
        query_cotangent, keyval_cotangent,
        master_query_up, master_keyval_up, master_query_down, master_keyval_down,
        mean_query_up, mean_keyval_up, mean_query_down, mean_keyval_down,
        square_query_up.reshape(1, 8), square_keyval_up.reshape(1, 8),
        square_query_down.reshape(1, QR), square_keyval_down.reshape(1, KR),
    )
    outs = pl.pallas_call(
        publish,
        name="publish",
        out_shape=tuple(jax.ShapeDtypeStruct(o.shape, o.dtype) for o in outs),
        in_specs=[hbm] * len(outs),
        out_specs=(hbm,) * len(outs),
        scratch_shapes=[V(o.shape, o.dtype) for o in outs]
        + [pltpu.SemaphoreType.DMA((len(outs),)), pltpu.SemaphoreType.DMA((len(outs),))],
    )(*outs)
    return (
        outs[0].T, *outs[1:9],
        outs[9].reshape(8), outs[10].reshape(8), outs[11].reshape(QR), outs[12].reshape(KR),
    )


def solution(mesh):
    both = P("dp", "head")
    return jax.shard_map(
        local,
        mesh=mesh,
        in_specs=(both, P("dp", None), P("dp", None), P(), P()) + (both,) * 10
        + (P("head"), P("head"), P("dp"), P("dp")),
        out_specs=(both,) * 9 + (P("head"), P("head"), P("dp"), P("dp")),
        check_vma=False,
    )
```
